128 devices in a mesh: dp: 32 (over y, x_lo, z), row: 2 (over x_hi), col: 2 (over core).
Axes of the slice: x: 4 (x_hi: 2, x_lo: 2; x = x_hi * 2 + x_lo), y: 4, z: 4, core: 2. Of those that a mesh axis runs over, the one named last changes fastest.
Arguments:
- tokens: bfloat16 [8192, 1024], P('dp', ('row', 'col')), may hold values from -6 to 6
- segment_ids: int32 [8192], P('dp'), may hold values from 0 to 31, as said below
- gain_one: float32 [1024], P(('row', 'col')), may hold values from 0.5 to 1.5
- in_weight: bfloat16 [1024, 3, 1024], P('row', None, 'col'), may hold values from -0.1875 to 0.1875
- conv_weight: bfloat16 [1024, 3], P(('col', 'row')), may hold values from -2.5 to 2.5
- out_weight: bfloat16 [1024, 1024], P('col', 'row'), may hold values from -0.1875 to 0.1875
- gain_two: float32 [1024], P(('row', 'col')), may hold values from 0.5 to 1.5
- gate_up: bfloat16 [1024, 2, 4608], P('row', None, 'col'), may hold values from -0.1875 to 0.1875
- down_weight: bfloat16 [4608, 1024], P('col', 'row'), may hold values from -0.125 to 0.125
- cotangent: bfloat16 [8192, 1024], P('dp', ('row', 'col')), may hold values from -6 to 6
Outputs:
- mixed: bfloat16 [8192, 1024], P('dp', ('row', 'col'))
- grad_tokens: bfloat16 [8192, 1024], P('dp', ('row', 'col'))
- grad_gain_one: float32 [1024], P(('row', 'col', 'dp'))
- grad_in: float32 [1024, 3, 1024], P(('row', 'dp'), None, 'col')
- grad_conv: float32 [1024, 3], P(('col', 'row', 'dp'))
- grad_out: float32 [1024, 1024], P(('col', 'dp'), 'row')
- grad_gain_two: float32 [1024], P(('row', 'col', 'dp'))
- grad_gate_up: float32 [1024, 2, 4608], P(('row', 'dp'), None, 'col')
- grad_down: float32 [4608, 1024], P(('col', 'dp'), 'row')
The draws below stay inside these ranges and needn't reach their ends.
Inputs may be any that keep to these rules, and one draw needn't show every extreme that they name: `segment_ids`: never falling, starting at 0, rising by 0 or 1 from one token to the next; it never rises at a position p with p % 256 below 2 or equal to 255.
All inputs are finite; a program needn't handle non-finite values.
Results may differ from the reference program's by a relative error of at most 0.035.
Values may be sent and summed in bfloat16 or wider, within the bound.
No kernel may reach another device: no remote copies, remote signals or barrier semaphores. Data moves between devices by JAX's collectives and lax.ppermute only.
A program may use at most 128 MiB of HBM per device.

```python
import jax
import jax.numpy as jnp
from jax import lax

D = 1024
FF = 4608
TOK_DEV = 256
TOKENS = 8192


def draw_segment_ids(key, part):
    key = jax.random.fold_in(key, 11)
    place = jnp.arange(TOKENS, dtype=jnp.int32)
    scores = jax.random.permutation(key, TOKENS).astype(jnp.int32)
    offset = place % TOK_DEV
    allowed = (offset >= 2) & (offset < TOK_DEV - 1)
    scores = jnp.where(allowed, scores, -1)
    picked = lax_top(scores, TOKENS // TOK_DEV - 1)
    starts = jnp.zeros((TOKENS,), jnp.int32).at[picked].set(1)
    return jnp.cumsum(starts).astype(jnp.int32)


def lax_top(scores, count):
    values, indices = jax.lax.top_k(scores, count)
    return indices.astype(jnp.int32)


def block_scale(own_key, dims, cuts, smallest, high):
    level, own = 1.0, jax.random.fold_in(own_key, 6)
    for axis_at, parts in cuts:
        heights = jnp.exp(jax.random.uniform(jax.random.fold_in(own, axis_at), (parts,), jnp.float32, smallest / len(cuts), high / len(cuts)))
        level = level * jnp.repeat(heights, dims[axis_at] // parts).reshape([-1 if axis == axis_at else 1 for axis in range(len(dims))])
    return level


def scatter_about(key, dims, spread, limit, split=(), kind=jnp.bfloat16):
    drawn = spread * jax.random.normal(key, dims, jnp.float32)
    if split:
        drawn = drawn * block_scale(key, dims, split, -0.22, 0.18)
    return jnp.clip(drawn, -limit, limit).astype(kind)


def setup_inputs(seed: int = 0) -> dict:
    key_list = jax.random.split(jax.random.key(seed), 11)
    return {
        "tokens": scatter_about(key_list[0], (TOKENS, D), 1.0, 6.0, ((0, 32), (1, 4))),
        "segment_ids": draw_segment_ids(jax.random.fold_in(key_list[10], 71), 0),
        "gain_one": jnp.clip(1.0 + 0.1 * jax.random.normal(key_list[2], (D,), jnp.float32), 0.5, 1.5),
        "in_weight": scatter_about(key_list[3], (D, 3, D), D ** -0.5, 0.1875, ((0, 2), (2, 2))),
        "conv_weight": scatter_about(key_list[4], (D, 3), 0.6, 2.5, ((0, 4),)),
        "out_weight": scatter_about(key_list[5], (D, D), D ** -0.5, 0.1875, ((0, 2), (1, 2))),
        "gain_two": jnp.clip(1.0 + 0.1 * jax.random.normal(key_list[6], (D,), jnp.float32), 0.5, 1.5),
        "gate_up": scatter_about(key_list[7], (D, 2, FF), D ** -0.5, 0.1875, ((0, 2), (2, 2))),
        "down_weight": scatter_about(key_list[8], (FF, D), (FF // 2) ** -0.5, 0.125, ((0, 2), (1, 2))),
        "cotangent": scatter_about(key_list[9], (TOKENS, D), 1.0, 6.0, ((0, 32), (1, 4))),
    }


@jax.custom_vjp
def low(v):
    return lax.optimization_barrier(v.astype(jnp.bfloat16)).astype(jnp.float32)

@jax.custom_vjp
def low_back(v):
    return v

def low_keep(v):
    return (low(v), None)

def low_pass(kept, grad):
    return (grad,)

def back_keep(v):
    return (v, None)

def back_low(kept, grad):
    return (low(grad),)
low.defvjp(low_keep, low_pass)
low_back.defvjp(back_keep, back_low)
eps_norm = 1e-05
best = lax.Precision.HIGHEST

def normed(value, gain):
    scale = lax.rsqrt(lax.optimization_barrier(jnp.mean(value * value, axis=-1, keepdims=True)) + eps_norm)
    return value * scale * gain

def reference(tokens, segment_ids, gain_one, in_weight, conv_weight, out_weight, gain_two, gate_up, down_weight, cotangent):
    seg_prev1 = jnp.concatenate([jnp.full((1,), -1, jnp.int32), segment_ids[:-1]])
    seg_prev2 = jnp.concatenate([jnp.full((2,), -1, jnp.int32), segment_ids[:-2]])
    same1 = (segment_ids == seg_prev1).astype(jnp.float32)[:, None]
    same2 = (segment_ids == seg_prev2).astype(jnp.float32)[:, None]

    def forward(x, g_one, w_in, w_conv, w_out, g_two, w_gu, w_down):
        n_one = low(normed(x, g_one))
        proj = low_back(jnp.einsum('td,dke->tke', n_one, w_in, precision=best))
        bx = low(proj[:, 0] * proj[:, 2])
        zeros_one = jnp.zeros((1, bx.shape[1]), jnp.float32)
        prev1 = jnp.concatenate([zeros_one, bx[:-1]])
        prev2 = jnp.concatenate([zeros_one, zeros_one, bx[:-2]])
        conv = w_conv[:, 2] * bx + w_conv[:, 1] * prev1 * same1 + w_conv[:, 0] * prev2 * same2
        ymix = low(proj[:, 1] * conv)
        out_part = low_back(jnp.dot(ymix, w_out, precision=best))
        hidden = x + out_part
        n_two = low(normed(hidden, g_two))
        gu = low_back(jnp.einsum('td,dke->tke', n_two, w_gu, precision=best))
        act = low(jax.nn.silu(gu[:, 0]) * gu[:, 1])
        ffn = low_back(jnp.dot(act, w_down, precision=best))
        return hidden + ffn
    inputs = (tokens.astype(jnp.float32), gain_one, in_weight.astype(jnp.float32), conv_weight.astype(jnp.float32), out_weight.astype(jnp.float32), gain_two, gate_up.astype(jnp.float32), down_weight.astype(jnp.float32))
    result, pullback = jax.vjp(forward, *inputs)
    grads = pullback(cotangent.astype(jnp.float32))
    return (result.astype(jnp.bfloat16), grads[0].astype(jnp.bfloat16), grads[1], grads[2], grads[3], grads[4], grads[5], grads[6], grads[7])
```

```python
import jax
import jax.numpy as jnp
from jax import lax
from jax.sharding import Mesh, PartitionSpec as P

eps_norm = 1e-05
f32 = jnp.float32
low = jnp.bfloat16
SIZES = {"y": 4, "xl": 2, "z": 4, "row": 2, "col": 2}
AXES = tuple(SIZES)


def moved(value, axes, place):
    sizes = [SIZES[a] for a in axes]
    pairs = []
    count = 1
    for size in sizes:
        count *= size
    for source in range(count):
        rest, coords = source, []
        for size in reversed(sizes):
            coords.insert(0, rest % size)
            rest //= size
        target = place(*coords)
        if target is None:
            continue
        index = 0
        for size, at in zip(sizes, target):
            index = index * size + at
        pairs.append((source, index))
    return lax.ppermute(value, axes if len(axes) > 1 else axes[0], pairs)


def ring(value, k):
    return moved(value, ("xl", "row"), lambda xl, row: (xl ^ (k & 1), row ^ (k >> 1)))


def swap_core(value):
    return moved(value, ("col",), lambda col: (1 - col,))


def dot(a, b, dims):
    return lax.dot_general(a, b, (dims, ((), ())), preferred_element_type=f32)


def mm(a, b):
    return dot(a, b, ((1,), (0,)))


def mm_t(a, b):
    return dot(a, b, ((1,), (1,)))


def t_mm(a, b):
    return dot(a, b, ((0,), (0,)))


def by_core(col, near, far):
    first = col == 0
    return jnp.where(first, near, far), jnp.where(first, far, near)


def gather8(piece, col):
    near = jnp.stack([piece] + [ring(piece, k) for k in (1, 2, 3)])
    both = jnp.concatenate(by_core(col, near, swap_core(near)), axis=-1)
    return both.reshape(2, 512, 512)


def reduce_core(part, col):
    part = jnp.stack(part)
    keep, send = by_core(col, part[..., :256], part[..., 256:])
    return (keep + swap_core(send.astype(low)).astype(f32)).reshape(4, 256, 256)


def reduce_ring(mine):
    sent = mine.astype(low)
    return mine[0] + sum(ring(sent[k], k).astype(f32) for k in (1, 2, 3))


def local(
    tokens,
    segment_ids,
    gain_one,
    in_weight,
    conv_weight,
    out_weight,
    gain_two,
    gate_up,
    down_weight,
    cotangent,
):
    yy, xl, zz, row, col = (lax.axis_index(a) for a in AXES)
    q = 2 * row + xl

    def cut(value, index, size, axis):
        return lax.dynamic_slice_in_dim(value, index * size, size, axis)

    def own(value):
        return cut(value, col, 256, value.ndim - 1)

    x = gather8(tokens, col).astype(f32)
    w_in = (cut(in_weight, q, 128, 2), ring(cut(in_weight, 3 - q, 128, 2), 3))
    gains = jnp.stack([gain_one, gain_two])
    gains = jnp.concatenate(by_core(col, gains, swap_core(gains)), axis=-1)
    gains = jnp.stack([gains, ring(gains, 2)])
    g_one, g_two = gains[:, 0][:, None, :], gains[:, 1][:, None, :]
    segs = jnp.stack([segment_ids, ring(segment_ids, 1)])

    def ordered(index):
        return jnp.concatenate([cut(out_weight, index ^ k, 128, 0) for k in range(4)])

    out_pair = (ordered(q), ring(ordered(3 - q), 3))
    w_out = [jnp.concatenate([w, swap_core(w)]) for w in out_pair]
    w_gu = (cut(gate_up, q, 576, 2), ring(cut(gate_up, 3 - q, 576, 2), 3))
    w_down = (cut(down_weight, q, 576, 0), ring(cut(down_weight, 3 - q, 576, 0), 3))
    df = gather8(cotangent, col)

    r_one = lax.rsqrt(jnp.sum(x * x, axis=(0, 2)) / 1024 + eps_norm)[:, None]
    n_one = (x * r_one * g_one).astype(low)
    proj = sum(dot(n_one[i], w_in[i], ((1,), (0,))) for i in (0, 1))
    blocks = proj.reshape(2, 256, 3, 128)
    b_val, c_val, u_val = blocks[:, :, 0], blocks[:, :, 1], blocks[:, :, 2]
    bx_low = (b_val * u_val).astype(low)

    def flip(value):
        return jnp.where(xl == 0, value, value[::-1])

    tails = flip(bx_low[:, 254:])
    prior = moved(tails, ("z",), lambda z: ((z + 1) % 4,))
    first = moved(
        tails[1], ("y", "z"), lambda y, z: (y + 1, 0) if z == 3 and y < 3 else None
    )
    start = zz == 0
    rim = flip(jnp.stack([jnp.where(start, first, prior[0]), jnp.where(start, prior[0], prior[1])]))
    extended = jnp.concatenate([rim, bx_low], axis=1).astype(f32)
    padded = jnp.concatenate([segs[:, :1], segs[:, :1], segs], axis=1)
    same_one = (segs == padded[:, 1:-1]).astype(f32)[:, :, None]
    same_two = (segs == padded[:, :-2]).astype(f32)[:, :, None]
    taps = cut(conv_weight, xl, 128, 0).astype(f32)
    conv = (
        taps[:, 2] * extended[:, 2:]
        + taps[:, 1] * extended[:, 1:-1] * same_one
        + taps[:, 0] * extended[:, :-2] * same_two
    )
    ymix = (c_val * conv).astype(low)
    y_swap = ymix[::-1].reshape(512, 128)
    ymix = ymix.reshape(512, 128)
    near = jnp.concatenate(
        [ymix, ring(y_swap, 1), ring(ymix, 2), ring(y_swap, 3)], axis=1
    )
    y_all = jnp.concatenate([near, swap_core(near)], axis=1)
    hidden = x + jnp.stack([mm(y_all, w_out[i]) for i in (0, 1)])

    r_two = lax.rsqrt(jnp.sum(hidden * hidden, axis=(0, 2)) / 1024 + eps_norm)[:, None]
    n_two = (hidden * r_two * g_two).astype(low)
    gu = sum(dot(n_two[i], w_gu[i], ((1,), (0,))) for i in (0, 1))
    gate, up_val = gu[:, 0], gu[:, 1]
    sig = jax.nn.sigmoid(gate)
    act = (gate * sig * up_val).astype(low)
    dact = sum(mm_t(df[i], w_down[i]) for i in (0, 1))
    dgu = jnp.stack(
        [dact * up_val * sig * (1.0 + gate * (1.0 - sig)), dact * gate * sig], axis=1
    ).astype(low)
    dn_two = [dot(dgu, w_gu[i], ((1, 2), (1, 2))) for i in (0, 1)]
    dn_two_own = reduce_ring(reduce_core(dn_two, col)).astype(low)
    dn_two = gather8(dn_two_own, col).astype(f32)
    h_own = own(hidden[0, :256])
    ffn_own = reduce_ring(reduce_core([mm(act, w_down[i]) for i in (0, 1)], col))
    mixed = (h_own + ffn_own).astype(low)

    dw_gu = [
        lax.psum_scatter(
            t_mm(n_two[i], dgu).astype(low), ("y", "z"), scatter_dimension=0, tiled=True
        )
        for i in (0, 1)
    ]
    dw_down = jnp.concatenate([t_mm(act, df[i]) for i in (0, 1)]).astype(low)
    dw_down = lax.psum_scatter(dw_down, ("y", "z"), scatter_dimension=0, tiled=True)

    def settle(value):
        return moved(
            value,
            ("y", "xl", "z", "row"),
            lambda y, xl, z, r: (2 * r + xl, y % 2, z, r ^ (y // 2)),
        ).astype(f32)

    spot = 2 * row + zz % 2

    def spread(pick):
        got = jnp.stack(
            [
                moved(
                    pick(j >> 1, xl ^ (j & 1)),
                    ("y", "xl", "z", "row"),
                    lambda y, xl, z, r, j=j: (
                        y,
                        z // 2,
                        2 * (z % 2) + (xl ^ (j & 1)),
                        r ^ (j >> 1),
                    ),
                )
                for j in range(4)
            ]
        )
        return [lax.dynamic_index_in_dim(got, spot ^ k, 0, keepdims=False) for k in range(4)]

    gu_got = spread(lambda i, half: cut(dw_gu[i], half, 16, 0))
    grad_gate_up = jnp.concatenate(gu_got, axis=-1).astype(f32)
    grad_down = settle(dw_down)

    total_two = jnp.sum(dn_two * g_two * hidden, axis=(0, 2))[:, None]
    dh = (
        df.astype(f32) + r_two * g_two * dn_two - hidden * r_two**3 * total_two / 1024
    )
    dg_two = jnp.sum(dn_two_own.astype(f32) * h_own * r_two[:256], axis=0)

    do_low = dh.astype(low)
    dymix = sum(mm_t(do_low[i], w_out[i][:128]) for i in (0, 1)).reshape(2, 256, 128)
    dw_out = jnp.concatenate([t_mm(ymix, do_low[i]) for i in (0, 1)]).astype(low)
    dconv = dymix * c_val
    dc_val = dymix * conv
    edge_one = dconv * same_one
    edge_two = dconv * same_two
    heads = flip(jnp.stack([edge_one[:, :2], edge_two[:, :2]], axis=1))
    later = moved(heads, ("z",), lambda z: ((z - 1) % 4,))
    last = moved(
        heads[0], ("y", "z"), lambda y, z: (y - 1, 3) if z == 0 and y > 0 else None
    )
    end = zz == 3
    rim_back = flip(jnp.stack([jnp.where(end, later[1], later[0]), jnp.where(end, last, later[1])]))
    ext_one = jnp.concatenate([edge_one, rim_back[:, 0]], axis=1)
    ext_two = jnp.concatenate([edge_two, rim_back[:, 1]], axis=1)
    dbx = taps[:, 2] * dconv + taps[:, 1] * ext_one[:, 1:257] + taps[:, 0] * ext_two[:, 2:258]
    dw_conv = jnp.stack(
        [
            jnp.sum(edge_two * extended[:, :-2], axis=(0, 1)),
            jnp.sum(edge_one * extended[:, 1:-1], axis=(0, 1)),
            jnp.sum(dconv * extended[:, 2:], axis=(0, 1)),
        ]
    )
    dproj = (
        jnp.stack([dbx * u_val, dc_val, dbx * b_val], axis=2).astype(low).reshape(512, 3, 128)
    )
    total_one = jnp.sum(dproj.astype(f32) * proj, axis=(1, 2)).reshape(2, 256)
    total_one = total_one + swap_core(total_one)
    total_one = total_one[0] + sum(ring(total_one[k & 1], k) for k in (1, 2, 3))
    dn_one = [dot(dproj, w_in[i], ((1, 2), (1, 2))) for i in (0, 1)]
    dn_one = reduce_core(dn_one, col)
    x_half = own(x)
    dg_one = jnp.sum(dn_one.reshape(2, 512, 256) * x_half * r_one, axis=1)
    dn_one = reduce_ring(dn_one)
    dw_in = jnp.stack([t_mm(n_one[i], dproj) for i in (0, 1)]).astype(low)

    zero = jnp.zeros((256,), f32)
    conv_pad = [
        jnp.where(xl == 0, jnp.concatenate([w, zero[:128]]), jnp.concatenate([zero[:128], w]))
        for w in dw_conv
    ]
    small = jnp.stack(
        [
            jnp.stack([dg_one[0], dg_two] + conv_pad),
            jnp.stack([dg_one[1], zero, zero, zero, zero]),
        ]
    ).astype(low)
    small = small.reshape(2, 5, 16, 2, 8).transpose(2, 0, 3, 1, 4)
    small = jnp.pad(small, ((0, 0), (0, 0), (0, 0), (0, 3), (0, 120)))
    in_part = dw_in.reshape(2, 16, 2, 16, 3, 128).transpose(1, 0, 2, 4, 3, 5)
    in_part = jnp.concatenate([in_part.reshape(16, 2, 2, 48, 128), small], axis=3)
    out_part = dw_out.reshape(16, 16, 4, 128).transpose(0, 2, 1, 3).reshape(16, 64, 128)
    late = jnp.concatenate([in_part.reshape(16, 224, 128), out_part], axis=1)
    late = lax.all_to_all(late, ("y", "z"), 0, 0)
    late = jnp.sum(late.astype(f32), axis=0).astype(low)
    out_got = late[224:].reshape(4, 16, 128).transpose(1, 0, 2).reshape(16, 512)
    grad_out = settle(out_got)
    in_late = late[:224].reshape(2, 2, 56, 128)
    in_got = spread(lambda i, half: lax.dynamic_index_in_dim(in_late[i], half, 0, keepdims=False))
    grad_in = jnp.concatenate(
        [w[:48].reshape(3, 16, 128).transpose(1, 0, 2) for w in in_got], axis=-1
    ).astype(f32)
    small = sum(w[48:].astype(f32) for w in in_got)[:5, :8]

    dx_val = (
        own(dh[0, :256])
        + r_one[:256] * own(g_one[0]) * dn_one
        - own(x[0, :256]) * r_one[:256] ** 2 * total_one[:, None] / 1024
    )
    return (
        mixed,
        dx_val.astype(low),
        small[0],
        grad_in,
        small[2:5].T,
        grad_out,
        small[1],
        grad_gate_up,
        grad_down,
    )


def solution(mesh):
    dp = ("y", "xl", "z")
    fine = Mesh(mesh.devices.reshape(tuple(SIZES.values())), AXES)
    return jax.shard_map(
        local,
        mesh=fine,
        in_specs=(
            P(dp, ("row", "col")),
            P(dp),
            P(("row", "col")),
            P("row", None, "col"),
            P(("col", "row"), None),
            P("col", "row"),
            P(("row", "col")),
            P("row", None, "col"),
            P("col", "row"),
            P(dp, ("row", "col")),
        ),
        out_specs=(
            P(dp, ("row", "col")),
            P(dp, ("row", "col")),
            P(("row", "col", *dp)),
            P(("row", *dp), None, "col"),
            P(("col", "row", *dp), None),
            P(("col", *dp), "row"),
            P(("row", "col", *dp)),
            P(("row", *dp), None, "col"),
            P(("col", *dp), "row"),
        ),
        check_vma=False,
    )
```

```python
import functools

import jax
import jax.numpy as jnp
from jax import lax
from jax.experimental import pallas as pl
from jax.experimental.pallas import tpu as pltpu
from jax.sharding import Mesh, PartitionSpec as P

eps_norm = 1e-05
f32 = jnp.float32
low = jnp.bfloat16
SIZES = {"y": 4, "xl": 2, "z": 4, "row": 2, "col": 2}
AXES = tuple(SIZES)


def moved(value, axes, place):
    sizes = [SIZES[a] for a in axes]
    pairs = []
    count = 1
    for size in sizes:
        count *= size
    for source in range(count):
        rest, coords = source, []
        for size in reversed(sizes):
            coords.insert(0, rest % size)
            rest //= size
        target = place(*coords)
        if target is None:
            continue
        index = 0
        for size, at in zip(sizes, target):
            index = index * size + at
        pairs.append((source, index))
    return lax.ppermute(value, axes if len(axes) > 1 else axes[0], pairs)


def ring(value, k):
    return moved(value, ("xl", "row"), lambda xl, row: (xl ^ (k & 1), row ^ (k >> 1)))


def swap_core(value):
    return moved(value, ("col",), lambda col: (1 - col,))


def dot(a, b, dims):
    return lax.dot_general(a, b, (dims, ((), ())), preferred_element_type=f32)


def mm(a, b):
    return dot(a, b, ((1,), (0,)))


def mm_t(a, b):
    return dot(a, b, ((1,), (1,)))


def lanes(index, size):
    return pl.ds(pl.multiple_of(index * size, size), size)


def rows(index, size):
    return pl.ds(pl.multiple_of(index * size, size), size)


def shaped(*shape, kind=f32):
    return jax.ShapeDtypeStruct(shape, kind)


def call(body, outs, scratch, place, *args):
    spec = pl.BlockSpec(memory_space=pltpu.VMEM)
    return pl.pallas_call(
        body,
        out_shape=outs,
        in_specs=[pl.BlockSpec(memory_space=pltpu.SMEM)] + [spec] * len(args),
        out_specs=[spec] * len(outs),
        scratch_shapes=scratch,
        compiler_params=pltpu.CompilerParams(vmem_limit_bytes=56 * 2**20),
    )(place, *args)


def turn(row):
    return jnp.broadcast_to(row, (128, 256)).T


def assemble(out, row, col, near, far):
    for k in range(4):
        at = (row ^ (k >> 1)) * 2
        here = slice((k & 1) * 256, (k & 1) * 256 + 256)
        out[here, lanes(at + col, 256)] = near[k][:256]
        out[here, lanes(at + 1 - col, 256)] = far[k][:256]


def norm_scale(value):
    return lax.rsqrt(jnp.sum(value * value, axis=1, keepdims=True) / 1024 + eps_norm)


def front(place, *refs):
    near, far, w_own = refs[0:4], refs[4:8], refs[8]
    x, n, gain, b, c, u, bx, tails, tail, same_one, same_two, w_far = refs[9:]
    row, xl, col = place[0], place[1], place[2]
    assemble(x, row, col, near, far)
    for k in (0, 2):
        for piece, at in ((near[k], col), (far[k], 1 - col)):
            extra = piece[256:272].astype(f32)
            for i in (0, 1):
                total = extra[3 * i : 3 * i + 1] + extra[3 * i + 1 : 3 * i + 2] + extra[3 * i + 2 : 3 * i + 3]
                gain[8 * i : 8 * i + 8, lanes((row ^ (k >> 1)) * 2 + at, 256)] = jnp.broadcast_to(total, (8, 256))
    for i in (0, 1):
        ids = turn(near[i][256:272].astype(f32)[6:7])
        one = jnp.concatenate([ids[:1], ids[:-1]])
        two = jnp.concatenate([ids[:1], ids[:1], ids[:-2]])
        same_one[256 * i : 256 * i + 256] = jnp.where(ids == one, 1.0, 0.0)
        same_two[256 * i : 256 * i + 256] = jnp.where(ids == two, 1.0, 0.0)

    @pl.loop(0, 8)
    def _(i):
        v = x[rows(i, 64)].astype(f32)
        n[rows(i, 64)] = (v * norm_scale(v) * gain[0:1]).astype(low)

    for i in range(3):
        for e in (0, 1):
            w_far[i, 256 * e : 256 * e + 256] = near[3][272 + 256 * i : 528 + 256 * i, 128 * e : 128 * e + 128]
    n_own, n_far = n[:, lanes(row, 512)], n[:, lanes(1 - row, 512)]
    for i, out in enumerate((b, c, u)):
        out[...] = mm(n_own, w_own[i]) + mm(n_far, w_far[i])
    bx[...] = (b[...] * u[...]).astype(low)
    ends = bx[240:256].astype(f32)[8:], bx[496:512].astype(f32)[8:]
    first = xl == 0
    tails[0] = jnp.where(first, ends[0], ends[1])
    tails[1] = jnp.where(first, ends[1], ends[0])
    tail[...] = jnp.where(first, ends[1], ends[0])


def conv_forward(place, bx, prior, first, c, same_one, same_two, taps, conv, y, y_swap, past_one, past_two):
    xl, zz = place[1], place[4]
    start = zz == 0
    rim = jnp.where(start, first[...], prior[0]), jnp.where(start, prior[0], prior[1])
    for i in (0, 1):
        here = slice(256 * i, 256 * i + 256)
        there = slice(256 - 256 * i, 512 - 256 * i)
        v = bx[here].astype(f32)
        ext = jnp.concatenate([jnp.where(xl == i, rim[0], rim[1]), v])
        one = ext[7:263] * same_one[here]
        two = ext[6:262] * same_two[here]
        past_one[here] = one
        past_two[here] = two
        total = taps[2:3] * v + taps[1:2] * one + taps[0:1] * two
        conv[here] = total
        mixed = (c[here] * total).astype(low)
        y[here] = mixed
        y_swap[there] = mixed


def feed(place, *refs):
    near, far = refs[0:4], refs[4:8]
    x, gain, out_own, out_swap, gu_own, down_own = refs[8:14]
    df_near, df_far, packs = refs[14:18], refs[18:22], refs[22]
    hidden, n, act, dgate, dup, keep, send, df, down_far, out_row = refs[23:33]
    y, wide, gate, up, dact, gu_far, out_far = refs[33:]
    row, xl, col = place[0], place[1], place[2]
    q = 2 * row + xl
    for m in range(16):
        for k in (0, 1):
            for t in range(5):
                at = (5 * k + t) * 32
                gu_far[k, 32 * m : 32 * m + 32, 128 * t : 128 * t + 128] = packs[m, at : at + 32]
        for t in range(4):
            first = 16 * (5 * m // 2)
            at = 320 + 48 * t
            down_far[first : first + 48, 128 * t : 128 * t + 128] = packs[m, at : at + 48]
            for e in (0, 1):
                at = 512 + (4 * e + t) * 32
                out_far[512 * e + 32 * m : 512 * e + 32 * m + 32, 128 * t : 128 * t + 128] = packs[m, at : at + 32]
    out_row[...] = out_far[rows(q, 128)]
    for k in range(4):
        y[:, lanes(col * 4 + (q ^ k), 128)] = near[k][...]
        y[:, lanes((1 - col) * 4 + (q ^ k), 128)] = far[k][...]
    assemble(df, row, col, df_near, df_far)
    y_own, y_far = y[:, lanes(col, 512)], y[:, lanes(1 - col, 512)]
    wide[:, lanes(row, 512)] = mm(y_own, out_own[...]) + mm(y_far, out_swap[...])
    wide[:, lanes(1 - row, 512)] = mm(y_own, out_far[:512]) + mm(y_far, out_far[512:])

    @pl.loop(0, 8)
    def _(i):
        h = x[rows(i, 64)].astype(f32) + wide[rows(i, 64)]
        hidden[rows(i, 64)] = h
        n[rows(i, 64)] = (h * norm_scale(h) * gain[8:9]).astype(low)

    n_own, n_far = n[:, lanes(row, 512)], n[:, lanes(1 - row, 512)]
    gate[...] = mm(n_own, gu_own[0]) + mm(n_far, gu_far[0])
    up[...] = mm(n_own, gu_own[1]) + mm(n_far, gu_far[1])
    dact[...] = mm_t(df[:, lanes(row, 512)], down_own[...]) + mm_t(df[:, lanes(1 - row, 512)], down_far[...])
    lane = lax.broadcasted_iota(jnp.int32, (64, 640), 1) - 64 * xl
    mine = (lane >= 0) & (lane < 576)

    @pl.loop(0, 8)
    def _(i):
        at = rows(i, 64)
        g = jnp.where(mine, gate[at], 0.0)
        v = jnp.where(mine, up[at], 0.0)
        da = dact[at]
        s = 1.0 / (1.0 + jnp.exp(-g))
        gs = g * s
        act[at] = (gs * v).astype(low)
        dgate[at] = (da * v * s * (1.0 + g * (1.0 - s))).astype(low)
        dup[at] = (da * gs).astype(low)

    for k, w in ((0, gu_own), (1, gu_far)):
        wide[:, 512 * k : 512 * k + 512] = mm_t(dgate[...], w[0]) + mm_t(dup[...], w[1])
    part(wide, keep, send, col)


def part(wide, keep, send, col):
    for k in range(4):
        here = slice(256 * (k & 1), 256 * (k & 1) + 256)
        keep[k] = wide[here, lanes(2 * (k >> 1) + col, 256)]
        send[k, :256] = wide[here, lanes(2 * (k >> 1) + 1 - col, 256)].astype(low)


def feed_weights(place, n, act, dgate, dup, df, down_own, down_far, early, keep, send, wide):
    row, xl, col = place[0], place[1], place[2]
    for k, w in ((0, down_own), (1, down_far)):
        wide[:512, 512 * k : 512 * k + 512] = mm(act[...], w[...])
    part(wide, keep, send, col)
    n_t = n[...].T
    for k, g in ((0, dgate), (1, dup)):
        for r in (0, 1):
            total = mm(n_t[512 * r : 512 * r + 512], g[...]).astype(low)
            for m in range(16):
                for t in range(5):
                    at = ((r * 2 + k) * 5 + t) * 32
                    early[m, at : at + 32] = total[32 * m : 32 * m + 32, 128 * t : 128 * t + 128]
    wide[...] = mm(act[...].T, df[...])
    for i in range(8):
        some = wide[pl.ds(pl.multiple_of(64 * xl + 72 * i, 8), 72)]
        some = jnp.concatenate([some, jnp.zeros((8, 1024), f32)]).astype(low)
        for r in (0, 1):
            for t in range(4):
                early[8 * r + i, 640 + 80 * t : 720 + 80 * t] = some[:, 512 * r + 128 * t : 512 * r + 128 * t + 128]


def fold(place, keep, got, own, *others):
    own[...] = keep[0] + got[0].astype(f32)
    for k in (1, 2, 3):
        others[k - 1][...] = (keep[k] + got[k].astype(f32)).astype(low)


def mix_backward(place, *refs):
    near, far = refs[0:4], refs[4:8]
    hidden, df, gain, w_own, w_far, c, conv, same_one, same_two = refs[8:17]
    dh_own, do, dconv, dc, heads, head, dg_two = refs[17:24]
    (dn,) = refs[24:]
    row, xl, col = place[0], place[1], place[2]
    assemble(dn, row, col, near, far)
    own = lanes(2 * row + col, 256)
    dg_two[...] = jnp.zeros((8, 256), f32)

    @pl.loop(0, 8)
    def _(i):
        at = rows(i, 64)
        h = hidden[at]
        r = norm_scale(h)
        d = dn[at].astype(f32)
        scaled = d * gain[8:9]
        total = jnp.sum(scaled * h, axis=1, keepdims=True)
        dh = df[at].astype(f32) + r * scaled - h * (r * r * r * total / 1024)
        do[at] = dh.astype(low)

        @pl.when(i < 4)
        def _():
            h = hidden[at, own]
            d = dn[at, own].astype(f32)
            dh_own[at] = df[at, own].astype(f32) + r * d * gain[8:9, own] - h * (r * r * r * total / 1024)
            dg_two[...] += jnp.broadcast_to(jnp.sum(d * h * r, axis=0, keepdims=True), (8, 256))

    dy = mm_t(do[:, lanes(row, 512)], w_own[...]) + mm_t(do[:, lanes(1 - row, 512)], w_far[...])
    edge = dy * c[...]
    dconv[...] = edge
    dc[...] = dy * conv[...]
    ends = [
        jnp.concatenate([edge[at : at + 8] * same_one[at : at + 8], edge[at : at + 8] * same_two[at : at + 8]])
        for at in (0, 256)
    ]
    first = xl == 0
    heads[0] = jnp.where(first, ends[0], ends[1])
    heads[1] = jnp.where(first, ends[1], ends[0])
    head[...] = jnp.where(first, ends[0], ends[1])


def conv_backward(place, *refs):
    dconv, dc, later, last, same_one, same_two, taps, b, c, u, past_one, past_two, bx, w_own, w_far = refs[:15]
    dproj, keep, send, total, grad_conv = refs[15:20]
    (wide,) = refs[20:]
    xl, col, zz = place[1], place[2], place[4]
    end = zz == 3
    rim = jnp.where(end, later[1], later[0]), jnp.where(end, last[...], later[1])
    parts = []
    for i in (0, 1):
        here = slice(256 * i, 256 * i + 256)
        d = dconv[here]
        edge = jnp.where(xl == i, rim[0], rim[1])
        one = jnp.concatenate([d * same_one[here], edge[:8]])
        two = jnp.concatenate([d * same_two[here], edge[8:]])
        dbx = taps[2:3] * d + taps[1:2] * one[1:257] + taps[0:1] * two[2:258]
        parts.append(jnp.concatenate([
            jnp.sum(d * past_two[here], axis=0, keepdims=True),
            jnp.sum(d * past_one[here], axis=0, keepdims=True),
            jnp.sum(d * bx[here].astype(f32), axis=0, keepdims=True),
            jnp.zeros((5, 128), f32),
        ]))
        db = (dbx * u[here]).astype(low)
        dcv = dc[here].astype(low)
        du = (dbx * b[here]).astype(low)
        dproj[here, 0:128] = db
        dproj[here, 128:256] = dcv
        dproj[here, 256:384] = du
        mass = jnp.sum(
            db.astype(f32) * b[here] + dcv.astype(f32) * c[here] + du.astype(f32) * u[here], axis=1, keepdims=True
        )
        line = jnp.broadcast_to(mass, (256, 128)).T[:8]
        total[i] = line
        high = line.astype(low)
        rest = (line - high.astype(f32)).astype(low)
        both = jnp.concatenate([high, rest])
        send[i, 256:272] = both
        send[2 + i, 256:272] = both
    grad_conv[...] = parts[0] + parts[1]
    for k, w in ((0, w_own), (1, w_far)):
        whole = jnp.concatenate([w[0], w[1], w[2]], axis=1)
        wide[:, 512 * k : 512 * k + 512] = mm_t(dproj[...], whole)
    part(wide, keep, send, col)


def mix_weights(place, n, dproj, y, do, small, late):
    n_t = n[...].T
    for r in (0, 1):
        total = mm(n_t[512 * r : 512 * r + 512], dproj[...]).astype(low)
        for m in range(16):
            for h in (0, 1):
                for k in range(3):
                    late[m, 2 * r + h, 16 * k : 16 * k + 16] = total[
                        32 * m + 16 * h : 32 * m + 16 * h + 16, 128 * k : 128 * k + 128
                    ]
                late[m, 2 * r + h, 48:64] = small[r]
    total = mm(y[...].T, do[...]).astype(low)
    for r in (0, 1):
        for i in range(8):
            for t in range(4):
                late[8 * r + i, 4, 16 * t : 16 * t + 16] = total[
                    16 * i : 16 * i + 16, 512 * r + 128 * t : 512 * r + 128 * t + 128
                ]


def fold_last(place, keep, got, keep_ffn, got_ffn, total, x, dg_two, grad_conv, own, own_ffn, mass, *rest):
    others, small = rest[:3], rest[3]
    row, xl, col = place[0], place[1], place[2]
    sums = [jnp.zeros((1, 256), f32), jnp.zeros((1, 256), f32)]
    scale = norm_scale(x[...].astype(f32))
    for k in range(4):
        whole = keep[k] + got[k, :256].astype(f32)
        line = total[k & 1] + got[k, 256:264].astype(f32) + got[k, 264:272].astype(f32)
        ffn = keep_ffn[k] + got_ffn[k].astype(f32)
        if k == 0:
            own[...] = whole
            own_ffn[...] = ffn
            mass[...] = line
        else:
            others[k - 1][272:528] = ffn.astype(low)
            others[k - 1][:256] = whole.astype(low)
            high = line.astype(low)
            others[k - 1][256:272] = jnp.concatenate([high, (line - high.astype(f32)).astype(low)])
        at = (k & 1) * 256
        v = x[at : at + 256, lanes((row ^ (k >> 1)) * 2 + col, 256)].astype(f32)
        sums[k >> 1] += jnp.sum(whole * v * scale[at : at + 256], axis=0, keepdims=True)
    zero = jnp.zeros((1, 128), f32)
    pair = lambda v: [v[:, :128], v[:, 128:]]
    taps = []
    for a in range(3):
        w = grad_conv[a : a + 1]
        taps += [jnp.where(xl == 0, w, zero), jnp.where(xl == 0, zero, w)]
    small[row] = jnp.concatenate(pair(sums[0]) + pair(dg_two[0:1]) + taps + [zero] * 6).astype(low)
    small[1 - row] = jnp.concatenate(pair(sums[1]) + [zero] * 14).astype(low)


def finish(place, own, own_ffn, mass, got1, got2, got3, dh, hidden, x, gain, out, mixed):
    row, col = place[0], place[2]
    here = lanes(2 * row + col, 256)
    total, line, ffn = own[...], mass[...], own_ffn[...]
    for got in (got1, got2, got3):
        total += got[:256].astype(f32)
        ffn += got[272:528].astype(f32)
        line += got[256:264].astype(f32) + got[264:272].astype(f32)
    scale = norm_scale(x[:256].astype(f32))
    column = turn(line[0:1])
    column = jnp.concatenate([column, column], axis=1)
    v = x[:256, here].astype(f32)
    mixed[...] = (hidden[...] + ffn).astype(low)
    out[...] = (dh[...] + scale * gain[0:1, here] * total - v * (scale * scale) * column / 1024).astype(low)


def local(
    tokens,
    segment_ids,
    gain_one,
    in_weight,
    conv_weight,
    out_weight,
    gain_two,
    gate_up,
    down_weight,
    cotangent,
):
    yy, xl, zz, row, col = (lax.axis_index(a) for a in AXES)
    q = 2 * row + xl
    place = jnp.stack([row, xl, col, yy, zz]).astype(jnp.int32)

    def cut(value, index, size, axis):
        return lax.dynamic_slice_in_dim(value, index * size, size, axis)

    def window(value, index, axis):
        return lax.dynamic_slice_in_dim(value, (9 * index // 2) * 128, 640, axis)

    extra = []
    for gain in (gain_one, gain_two):
        for _ in range(3):
            piece = lax.reduce_precision(gain, 8, 7)
            extra.append(piece)
            gain = gain - piece
    extra.append(segment_ids.astype(f32))
    extra = jnp.pad(jnp.stack(extra), ((0, 9), (0, 0))).astype(low)
    piece = jnp.concatenate([tokens, extra])
    in_w = in_weight.transpose(1, 0, 2)
    in_own, in_send = cut(in_w, q, 128, 2), cut(in_w, 3 - q, 128, 2)
    in_send = jnp.concatenate([in_send[:, :256], in_send[:, 256:]], axis=2).reshape(768, 256)
    near = [piece, ring(piece, 1), ring(piece, 2), ring(jnp.concatenate([piece, in_send]), 3)]
    far = [swap_core(v) for v in near[:3]] + [swap_core(near[3][:272])]
    taps = jnp.pad(cut(conv_weight, xl, 128, 0).T.astype(f32), ((0, 5), (0, 0)))

    def begin(index):
        return (9 * index // 2) * 128

    m = 4 * yy + zz
    gu_part = lax.dynamic_slice(gate_up, (32 * m, 0, begin(3 - q)), (32, 2, 640))
    gu_part = gu_part.reshape(32, 2, 5, 128).transpose(1, 2, 0, 3).reshape(320, 128)
    down_part = lax.dynamic_slice(down_weight, (begin(3 - q) + 16 * (5 * m // 2), 0), (48, 512))
    down_part = down_part.reshape(48, 4, 128).transpose(1, 0, 2).reshape(192, 128)
    out_part = cut(out_weight, m, 32, 0).reshape(32, 4, 128).transpose(1, 0, 2).reshape(128, 128)
    pack = ring(jnp.concatenate([gu_part, down_part, out_part]), 3)
    cross = moved(out_part, ("xl", "row", "col"), lambda xl, row, col: (1 - xl, 1 - row, 1 - col))
    packs = lax.all_gather(jnp.concatenate([pack, cross]), ("y", "z"))
    out_swap = swap_core(out_weight)
    gu_own, down_own = window(gate_up.transpose(1, 0, 2), q, 2), window(down_weight, q, 0)

    tile = shaped(512, 128)
    tile_low = shaped(512, 128, kind=low)
    whole_low = shaped(512, 1024, kind=low)
    x, n_one, gain, b, c, u, bx, tails, tail, same_one, same_two = call(
        front,
        [whole_low, whole_low, shaped(16, 1024), tile, tile, tile, tile_low, shaped(2, 8, 128), shaped(8, 128), tile, tile],
        [pltpu.VMEM((3, 512, 128), low)],
        place,
        *near,
        *far,
        in_own,
    )
    in_far = near[3][272:].reshape(3, 256, 2, 128).transpose(0, 2, 1, 3).reshape(3, 512, 128)
    df, tails = lax.optimization_barrier((cotangent, tails))
    df_near = [df] + [ring(df, k) for k in (1, 2, 3)]
    df_far = [swap_core(v) for v in df_near]
    prior = moved(tails, ("z",), lambda z: ((z + 1) % 4,))
    first = moved(tail, ("y", "z"), lambda y, z: (y + 1, 0) if z == 3 and y < 3 else None)
    conv, y, y_swap, past_one, past_two = call(
        conv_forward, [tile, tile_low, tile_low, tile, tile], [], place, bx, prior, first, c, same_one, same_two, taps
    )
    near = [y, ring(y_swap, 1), ring(y, 2), ring(y_swap, 3)]
    far = [swap_core(v) for v in near]

    hid_low = shaped(512, 640, kind=low)
    keep4, send4 = shaped(4, 256, 256), shaped(4, 256, 256, kind=low)
    send4_mass = shaped(4, 272, 256, kind=low)
    hidden, n_two, act, dgate, dup, keep, send, df, down_far, out_row = call(
        feed,
        [
            shaped(512, 1024),
            whole_low,
            hid_low,
            hid_low,
            hid_low,
            keep4,
            send4,
            whole_low,
            shaped(640, 512, kind=low),
            shaped(128, 512, kind=low),
        ],
        [
            pltpu.VMEM((512, 1024), low),
            pltpu.VMEM((512, 1024), f32),
            pltpu.VMEM((512, 640), f32),
            pltpu.VMEM((512, 640), f32),
            pltpu.VMEM((512, 640), f32),
            pltpu.VMEM((2, 512, 640), low),
            pltpu.VMEM((1024, 512), low),
        ],
        place,
        *near,
        *far,
        x,
        gain,
        out_weight,
        out_swap,
        gu_own,
        down_own,
        *df_near,
        *df_far,
        packs,
    )
    got = swap_core(send)
    own = shaped(256, 256)
    own_low = shaped(256, 256, kind=low)
    dn_own, *parts = call(fold, [own, own_low, own_low, own_low], [], place, keep, got)
    ringed = [ring(v, k) for k, v in zip((1, 2, 3), parts)]
    n_two, dn_own, *parts = lax.optimization_barrier((n_two, dn_own, *parts))
    early, keep_ffn, send_ffn = call(
        feed_weights,
        [shaped(16, 960, 128, kind=low), keep4, send4],
        [pltpu.VMEM((640, 1024), f32)],
        place,
        n_two,
        act,
        dgate,
        dup,
        df,
        down_own,
        down_far,
    )
    dn_own, early = lax.optimization_barrier((dn_own, early))
    early = early.reshape(16 * 960, 128)
    early = lax.psum_scatter(early, ("y", "z"), scatter_dimension=0, tiled=True)
    got_ffn = swap_core(send_ffn)
    piece = (dn_own + sum(v.astype(f32) for v in ringed)).astype(low)
    near = [piece] + [ring(piece, k) for k in (1, 2, 3)]
    far = [swap_core(v) for v in near]
    dh_own, do, dconv, dc, heads, head, dg_two = call(
        mix_backward,
        [own, whole_low, tile, tile, shaped(2, 16, 128), shaped(16, 128), shaped(8, 256)],
        [pltpu.VMEM((512, 1024), low)],
        place,
        *near,
        *far,
        hidden,
        df,
        gain,
        cut(out_weight, q, 128, 0),
        out_row,
        c,
        conv,
        same_one,
        same_two,
    )
    later = moved(heads, ("z",), lambda z: ((z - 1) % 4,))
    last = moved(head, ("y", "z"), lambda y, z: (y - 1, 3) if z == 0 and y > 0 else None)
    dproj, keep, send, total, grad_conv = call(
        conv_backward,
        [shaped(512, 384, kind=low), keep4, send4_mass, shaped(2, 8, 256), shaped(8, 128)],
        [pltpu.VMEM((512, 1024), f32)],
        place,
        dconv,
        dc,
        later,
        last,
        same_one,
        same_two,
        taps,
        b,
        c,
        u,
        past_one,
        past_two,
        bx,
        in_own,
        in_far,
    )
    got = swap_core(send)
    own_mass = shaped(528, 256, kind=low)
    dn_own, ffn_own, mass, *parts, small = call(
        fold_last,
        [own, own, shaped(8, 256), own_mass, own_mass, own_mass, shaped(2, 16, 128, kind=low)],
        [],
        place,
        keep,
        got,
        keep_ffn,
        got_ffn,
        total,
        x,
        dg_two,
        grad_conv,
    )
    (late,) = call(mix_weights, [shaped(16, 5, 64, 128, kind=low)], [], place, n_one, dproj, y, do, small)
    ringed = [ring(v, k) for k, v in zip((1, 2, 3), parts)]
    late = lax.all_to_all(late, ("y", "z"), 0, 0)
    h_own = lax.dynamic_slice_in_dim(hidden[:256], (2 * row + col) * 256, 256, 1)
    grad_tokens, mixed = call(
        finish, [own_low, own_low], [], place, dn_own, ffn_own, mass, *ringed, dh_own, h_own, x, gain
    )

    def settle(value):
        return moved(
            value,
            ("y", "xl", "z", "row"),
            lambda y, xl, z, r: (2 * r + xl, y % 2, z, y // 2),
        ).astype(f32)

    spot = 2 * row + zz % 2

    def spread(pick):
        got = jnp.stack(
            [
                moved(
                    pick(row ^ (j >> 1), xl ^ (j & 1)),
                    ("y", "xl", "z", "row"),
                    lambda y, xl, z, r, j=j: (y, z // 2, 2 * (z % 2) + (xl ^ (j & 1)), r ^ (j >> 1)),
                )
                for j in range(4)
            ]
        )
        return [lax.dynamic_index_in_dim(got, spot ^ k, 0, keepdims=False) for k in range(4)]

    gu_early = early[:640].reshape(2, 10, 2, 16, 128)
    down_early = early[640:].reshape(4, 80, 128)[:, :72].transpose(1, 0, 2).reshape(72, 512)
    gu_got = spread(lambda r, half: lax.dynamic_slice(gu_early, (r, 0, half, 0, 0), (1, 10, 1, 16, 128)).reshape(2, 5, 16, 128))
    gu_got = [w.astype(f32) for w in gu_got]
    grad_gate_up = jnp.concatenate(
        [
            gu_got[0][:, :4],
            gu_got[0][:, 4:] + gu_got[1][:, :1],
            gu_got[1][:, 1:],
            gu_got[2][:, :4],
            gu_got[2][:, 4:] + gu_got[3][:, :1],
            gu_got[3][:, 1:],
        ],
        axis=1,
    )
    grad_gate_up = grad_gate_up.transpose(2, 0, 1, 3).reshape(16, 2, 2304)
    grad_down = settle(down_early)

    late = jnp.sum(late.astype(f32), axis=0).astype(low)
    grad_out = settle(late[4].reshape(4, 16, 128).transpose(1, 0, 2).reshape(16, 512))
    in_got = spread(lambda r, half: lax.dynamic_index_in_dim(late, 2 * r + half, 0, keepdims=False))
    grad_in = jnp.concatenate(
        [w[:48].reshape(3, 16, 128).transpose(1, 0, 2) for w in in_got], axis=-1
    ).astype(f32)
    small = sum(w[48:].astype(f32) for w in in_got)[:10].reshape(5, 256)
    small = cut(small, 8 * yy + 4 * xl + zz, 8, 1)
    return (
        mixed,
        grad_tokens,
        small[0],
        grad_in,
        small[2:5].T,
        grad_out,
        small[1],
        grad_gate_up,
        grad_down,
    )


def solution(mesh):
    dp = ("y", "xl", "z")
    fine = Mesh(mesh.devices.reshape(tuple(SIZES.values())), AXES)
    return jax.shard_map(
        local,
        mesh=fine,
        in_specs=(
            P(dp, ("row", "col")),
            P(dp),
            P(("row", "col")),
            P("row", None, "col"),
            P(("col", "row"), None),
            P("col", "row"),
            P(("row", "col")),
            P("row", None, "col"),
            P("col", "row"),
            P(dp, ("row", "col")),
        ),
        out_specs=(
            P(dp, ("row", "col")),
            P(dp, ("row", "col")),
            P(("row", "col", *dp)),
            P(("row", *dp), None, "col"),
            P(("col", "row", *dp), None),
            P(("col", *dp), "row"),
            P(("row", "col", *dp)),
            P(("row", *dp), None, "col"),
            P(("col", *dp), "row"),
        ),
        check_vma=False,
    )
```

```python
import functools

import jax
import jax.numpy as jnp
from jax import lax
from jax.experimental import pallas as pl
from jax.experimental.pallas import tpu as pltpu
from jax.sharding import Mesh, PartitionSpec as P

eps_norm = 1e-05
f32 = jnp.float32
low = jnp.bfloat16
SIZES = {"y": 4, "xl": 2, "z": 4, "row": 2, "col": 2}
AXES = tuple(SIZES)


def moved(value, axes, place):
    sizes = [SIZES[a] for a in axes]
    pairs = []
    count = 1
    for size in sizes:
        count *= size
    for source in range(count):
        rest, coords = source, []
        for size in reversed(sizes):
            coords.insert(0, rest % size)
            rest //= size
        target = place(*coords)
        if target is None:
            continue
        index = 0
        for size, at in zip(sizes, target):
            index = index * size + at
        pairs.append((source, index))
    return lax.ppermute(value, axes if len(axes) > 1 else axes[0], pairs)


def ring(value, k):
    return moved(value, ("xl", "row"), lambda xl, row: (xl ^ (k & 1), row ^ (k >> 1)))


def swap_core(value):
    return moved(value, ("col",), lambda col: (1 - col,))


def dot(a, b, dims):
    return lax.dot_general(a, b, (dims, ((), ())), preferred_element_type=f32)


def mm(a, b):
    return dot(a, b, ((1,), (0,)))


def mm_t(a, b):
    return dot(a, b, ((1,), (1,)))


def lanes(index, size):
    return pl.ds(pl.multiple_of(index * size, size), size)


def rows(index, size):
    return pl.ds(pl.multiple_of(index * size, size), size)


def shaped(*shape, kind=f32):
    return jax.ShapeDtypeStruct(shape, kind)


def call(body, outs, scratch, place, *args):
    spec = pl.BlockSpec(memory_space=pltpu.VMEM)
    return pl.pallas_call(
        body,
        out_shape=outs,
        in_specs=[pl.BlockSpec(memory_space=pltpu.SMEM)] + [spec] * len(args),
        out_specs=[spec] * len(outs),
        scratch_shapes=scratch,
        compiler_params=pltpu.CompilerParams(vmem_limit_bytes=56 * 2**20),
    )(place, *args)


def turn(row):
    return jnp.broadcast_to(row, (128, 256)).T


def assemble(out, row, col, near, far):
    for k in range(4):
        at = (row ^ (k >> 1)) * 2
        here = slice((k & 1) * 256, (k & 1) * 256 + 256)
        out[here, lanes(at + col, 256)] = near[k][:256]
        out[here, lanes(at + 1 - col, 256)] = far[k][:256]


def norm_scale(value):
    return lax.rsqrt(jnp.sum(value * value, axis=1, keepdims=True) / 1024 + eps_norm)


def front(place, *refs):
    near, far, w_own = refs[0:4], refs[4:8], refs[8]
    x, n, gain, b, c, u, bx, tails, tail, same_one, same_two, scale, w_far = refs[9:]
    row, xl, col = place[0], place[1], place[2]
    assemble(x, row, col, near, far)
    for k in (0, 2):
        for piece, at in ((near[k], col), (far[k], 1 - col)):
            extra = piece[256:272].astype(f32)
            for i in (0, 1):
                total = extra[3 * i : 3 * i + 1] + extra[3 * i + 1 : 3 * i + 2] + extra[3 * i + 2 : 3 * i + 3]
                gain[8 * i : 8 * i + 8, lanes((row ^ (k >> 1)) * 2 + at, 256)] = jnp.broadcast_to(total, (8, 256))
    for i in (0, 1):
        ids = turn(near[i][256:272].astype(f32)[6:7])
        one = jnp.concatenate([ids[:1], ids[:-1]])
        two = jnp.concatenate([ids[:1], ids[:1], ids[:-2]])
        same_one[256 * i : 256 * i + 256] = jnp.where(ids == one, 1.0, 0.0)
        same_two[256 * i : 256 * i + 256] = jnp.where(ids == two, 1.0, 0.0)

    @pl.loop(0, 8)
    def _(i):
        v = x[rows(i, 64)].astype(f32)
        r = norm_scale(v)
        scale[rows(i, 64)] = jnp.broadcast_to(r, (64, 128))
        n[rows(i, 64)] = (v * r * gain[0:1]).astype(low)

    for i in range(3):
        for e in (0, 1):
            w_far[i, 256 * e : 256 * e + 256] = near[3][272 + 256 * i : 528 + 256 * i, 128 * e : 128 * e + 128]
    n_own, n_far = n[:, lanes(row, 512)], n[:, lanes(1 - row, 512)]
    for i, out in enumerate((b, c, u)):
        out[...] = mm(n_own, w_own[i]) + mm(n_far, w_far[i])
    bx[...] = (b[...] * u[...]).astype(low)
    ends = bx[240:256].astype(f32)[8:], bx[496:512].astype(f32)[8:]
    first = xl == 0
    tails[0] = jnp.where(first, ends[0], ends[1])
    tails[1] = jnp.where(first, ends[1], ends[0])
    tail[...] = jnp.where(first, ends[1], ends[0])


def conv_forward(place, bx, prior, first, c, same_one, same_two, taps, conv, y, y_swap, past_one, past_two):
    xl, zz = place[1], place[4]
    start = zz == 0
    rim = jnp.where(start, first[...], prior[0]), jnp.where(start, prior[0], prior[1])
    for i in (0, 1):
        here = slice(256 * i, 256 * i + 256)
        there = slice(256 - 256 * i, 512 - 256 * i)
        v = bx[here].astype(f32)
        ext = jnp.concatenate([jnp.where(xl == i, rim[0], rim[1]), v])
        one = ext[7:263] * same_one[here]
        two = ext[6:262] * same_two[here]
        past_one[here] = one
        past_two[here] = two
        total = taps[2:3] * v + taps[1:2] * one + taps[0:1] * two
        conv[here] = total
        mixed = (c[here] * total).astype(low)
        y[here] = mixed
        y_swap[there] = mixed


def feed(place, *refs):
    near, far = refs[0:4], refs[4:8]
    x, gain, out_own, out_swap, gu_own, down_own = refs[8:14]
    df_near, df_far, packs = refs[14:18], refs[18:22], refs[22]
    hidden, n, act, dgate, dup, keep, send, df, down_far, out_row = refs[23:33]
    y, wide, gate, up, dact, gu_far, out_far = refs[33:]
    row, xl, col = place[0], place[1], place[2]
    q = 2 * row + xl
    for m in range(16):
        for k in (0, 1):
            for t in range(5):
                at = (5 * k + t) * 32
                gu_far[k, 32 * m : 32 * m + 32, 128 * t : 128 * t + 128] = packs[m, at : at + 32]
        for t in range(4):
            first = 16 * (5 * m // 2)
            at = 320 + 48 * t
            down_far[first : first + 48, 128 * t : 128 * t + 128] = packs[m, at : at + 48]
            for e in (0, 1):
                at = 512 + (4 * e + t) * 32
                out_far[512 * e + 32 * m : 512 * e + 32 * m + 32, 128 * t : 128 * t + 128] = packs[m, at : at + 32]
    out_row[...] = out_far[rows(q, 128)]
    for k in range(4):
        y[:, lanes(col * 4 + (q ^ k), 128)] = near[k][...]
        y[:, lanes((1 - col) * 4 + (q ^ k), 128)] = far[k][...]
    assemble(df, row, col, df_near, df_far)
    y_own, y_far = y[:, lanes(col, 512)], y[:, lanes(1 - col, 512)]
    wide[:, lanes(row, 512)] = mm(y_own, out_own[...]) + mm(y_far, out_swap[...])
    wide[:, lanes(1 - row, 512)] = mm(y_own, out_far[:512]) + mm(y_far, out_far[512:])

    @pl.loop(0, 8)
    def _(i):
        h = x[rows(i, 64)].astype(f32) + wide[rows(i, 64)]
        hidden[rows(i, 64)] = h
        n[rows(i, 64)] = (h * norm_scale(h) * gain[8:9]).astype(low)

    n_own, n_far = n[:, lanes(row, 512)], n[:, lanes(1 - row, 512)]
    gate[...] = mm(n_own, gu_own[0]) + mm(n_far, gu_far[0])
    up[...] = mm(n_own, gu_own[1]) + mm(n_far, gu_far[1])
    dact[...] = mm_t(df[:, lanes(row, 512)], down_own[...]) + mm_t(df[:, lanes(1 - row, 512)], down_far[...])
    lane = lax.broadcasted_iota(jnp.int32, (64, 640), 1) - 64 * xl
    mine = (lane >= 0) & (lane < 576)

    @pl.loop(0, 8)
    def _(i):
        at = rows(i, 64)
        g = jnp.where(mine, gate[at], 0.0)
        v = jnp.where(mine, up[at], 0.0)
        da = dact[at]
        s = 1.0 / (1.0 + jnp.exp(-g))
        gs = g * s
        act[at] = (gs * v).astype(low)
        dgate[at] = (da * v * s * (1.0 + g * (1.0 - s))).astype(low)
        dup[at] = (da * gs).astype(low)

    for k, w in ((0, gu_own), (1, gu_far)):
        wide[:, 512 * k : 512 * k + 512] = mm_t(dgate[...], w[0]) + mm_t(dup[...], w[1])
    part(wide, keep, send, col)


def part(wide, keep, send, col):
    for k in range(4):
        here = slice(256 * (k & 1), 256 * (k & 1) + 256)
        keep[k] = wide[here, lanes(2 * (k >> 1) + col, 256)]
        send[k, :256] = wide[here, lanes(2 * (k >> 1) + 1 - col, 256)].astype(low)


def feed_out(place, act, down_own, down_far, keep, send, wide):
    for k, w in ((0, down_own), (1, down_far)):
        wide[:, 512 * k : 512 * k + 512] = mm(act[...], w[...])
    part(wide, keep, send, place[2])


def source_row(m, half):
    return 128 * (m // 4) + 64 * half + 16 * (m % 4)


def feed_weights(place, n, act, dgate, dup, df, early, wide):
    xl = place[1]
    n_t = n[...].T
    for k, g in ((0, dgate), (1, dup)):
        for r in (0, 1):
            total = mm(n_t[512 * r : 512 * r + 512], g[...]).astype(low)
            for m in range(16):
                for t in range(5):
                    for h in (0, 1):
                        at = ((r * 2 + k) * 5 + t) * 32 + 16 * h
                        first = source_row(m, h)
                        early[m, at : at + 16] = total[first : first + 16, 128 * t : 128 * t + 128]
    wide[...] = mm(act[...].T, df[...])
    for i in range(8):
        some = wide[pl.ds(pl.multiple_of(64 * xl + 72 * i, 8), 72)]
        some = jnp.concatenate([some, jnp.zeros((8, 1024), f32)]).astype(low)
        for r in (0, 1):
            for t in range(4):
                early[8 * r + i, 640 + 80 * t : 720 + 80 * t] = some[:, 512 * r + 128 * t : 512 * r + 128 * t + 128]


def fold(place, keep, got, own, *others):
    own[...] = keep[0] + got[0].astype(f32)
    for k in (1, 2, 3):
        others[k - 1][...] = (keep[k] + got[k].astype(f32)).astype(low)


def mix_backward(place, *refs):
    near, far = refs[0:4], refs[4:8]
    hidden, df, gain, w_own, w_far, c, conv, same_one, same_two = refs[8:17]
    dh_own, do, dconv, dc, heads, head, dg_two = refs[17:24]
    (dn,) = refs[24:]
    row, xl, col = place[0], place[1], place[2]
    assemble(dn, row, col, near, far)
    own = lanes(2 * row + col, 256)
    dg_two[...] = jnp.zeros((8, 256), f32)

    @pl.loop(0, 8)
    def _(i):
        at = rows(i, 64)
        h = hidden[at]
        r = norm_scale(h)
        d = dn[at].astype(f32)
        scaled = d * gain[8:9]
        total = jnp.sum(scaled * h, axis=1, keepdims=True)
        dh = df[at].astype(f32) + r * scaled - h * (r * r * r * total / 1024)
        do[at] = dh.astype(low)

        @pl.when(i < 4)
        def _():
            h = hidden[at, own]
            d = dn[at, own].astype(f32)
            dh_own[at] = df[at, own].astype(f32) + r * d * gain[8:9, own] - h * (r * r * r * total / 1024)
            dg_two[...] += jnp.broadcast_to(jnp.sum(d * h * r, axis=0, keepdims=True), (8, 256))

    dy = mm_t(do[:, lanes(row, 512)], w_own[...]) + mm_t(do[:, lanes(1 - row, 512)], w_far[...])
    edge = dy * c[...]
    dconv[...] = edge
    dc[...] = dy * conv[...]
    ends = [
        jnp.concatenate([edge[at : at + 8] * same_one[at : at + 8], edge[at : at + 8] * same_two[at : at + 8]])
        for at in (0, 256)
    ]
    first = xl == 0
    heads[0] = jnp.where(first, ends[0], ends[1])
    heads[1] = jnp.where(first, ends[1], ends[0])
    head[...] = jnp.where(first, ends[0], ends[1])


def conv_backward(place, *refs):
    dconv, dc, later, last, same_one, same_two, taps, b, c, u, past_one, past_two, bx, w_own, w_far = refs[:15]
    x, scale, dg_two = refs[15:18]
    dproj, keep, send, total, small = refs[18:23]
    (wide,) = refs[23:]
    row, xl, col, zz = place[0], place[1], place[2], place[4]
    end = zz == 3
    rim = jnp.where(end, later[1], later[0]), jnp.where(end, last[...], later[1])
    parts = []
    for i in (0, 1):
        here = slice(256 * i, 256 * i + 256)
        d = dconv[here]
        edge = jnp.where(xl == i, rim[0], rim[1])
        one = jnp.concatenate([d * same_one[here], edge[:8]])
        two = jnp.concatenate([d * same_two[here], edge[8:]])
        dbx = taps[2:3] * d + taps[1:2] * one[1:257] + taps[0:1] * two[2:258]
        parts.append(jnp.concatenate([
            jnp.sum(d * past_two[here], axis=0, keepdims=True),
            jnp.sum(d * past_one[here], axis=0, keepdims=True),
            jnp.sum(d * bx[here].astype(f32), axis=0, keepdims=True),
            jnp.zeros((5, 128), f32),
        ]))
        db = (dbx * u[here]).astype(low)
        dcv = dc[here].astype(low)
        du = (dbx * b[here]).astype(low)
        dproj[here, 0:128] = db
        dproj[here, 128:256] = dcv
        dproj[here, 256:384] = du
        mass = jnp.sum(
            db.astype(f32) * b[here] + dcv.astype(f32) * c[here] + du.astype(f32) * u[here], axis=1, keepdims=True
        )
        line = jnp.broadcast_to(mass, (256, 128)).T[:8]
        total[i] = line
        high = line.astype(low)
        rest = (line - high.astype(f32)).astype(low)
        both = jnp.concatenate([high, rest])
        send[i, 256:272] = both
        send[2 + i, 256:272] = both
    zero = jnp.zeros((1, 128), f32)
    for k, w in ((0, w_own), (1, w_far)):
        whole = jnp.concatenate([w[0], w[1], w[2]], axis=1)
        wide[:, 512 * k : 512 * k + 512] = mm_t(dproj[...], whole)
        sums = jnp.zeros((1, 512), f32)
        for i in range(8):
            here = slice(64 * i, 64 * i + 64)
            v = x[here, lanes(row ^ k, 512)].astype(f32)
            r = scale[here]
            r = jnp.concatenate([r, r, r, r], axis=1)
            sums += jnp.sum(wide[here, 512 * k : 512 * k + 512] * v * r, axis=0, keepdims=True)
        lines = [sums[:, 128 * t : 128 * t + 128] for t in range(4)]
        if k == 0:
            lines += [dg_two[0:1, :128], dg_two[0:1, 128:]]
            for a in range(3):
                tap = parts[0][a : a + 1] + parts[1][a : a + 1]
                lines += [jnp.where(xl == 0, tap, zero), jnp.where(xl == 0, zero, tap)]
        lines += [zero] * (16 - len(lines))
        small[row ^ k] = jnp.concatenate(lines).astype(low)
    part(wide, keep, send, col)


def mix_weights(place, n, dproj, y, do, small, late):
    n_t = n[...].T
    for r in (0, 1):
        total = mm(n_t[512 * r : 512 * r + 512], dproj[...]).astype(low)
        for m in range(16):
            for h in (0, 1):
                for k in range(3):
                    first = source_row(m, h)
                    late[m, 2 * r + h, 16 * k : 16 * k + 16] = total[first : first + 16, 128 * k : 128 * k + 128]
                late[m, 2 * r + h, 48:64] = small[r]
    total = mm(y[...].T, do[...]).astype(low)
    for r in (0, 1):
        for i in range(8):
            for t in range(4):
                late[8 * r + i, 4, 16 * t : 16 * t + 16] = total[
                    16 * i : 16 * i + 16, 512 * r + 128 * t : 512 * r + 128 * t + 128
                ]


def fold_last(place, keep, got, keep_ffn, got_ffn, total, own, own_ffn, mass, *others):
    for k in range(4):
        whole = keep[k] + got[k, :256].astype(f32)
        line = total[k & 1] + got[k, 256:264].astype(f32) + got[k, 264:272].astype(f32)
        ffn = keep_ffn[k] + got_ffn[k].astype(f32)
        if k == 0:
            own[...] = whole
            own_ffn[...] = ffn
            mass[...] = line
        else:
            others[k - 1][272:528] = ffn.astype(low)
            others[k - 1][:256] = whole.astype(low)
            high = line.astype(low)
            others[k - 1][256:272] = jnp.concatenate([high, (line - high.astype(f32)).astype(low)])


def finish(place, own, own_ffn, mass, got1, got2, got3, dh, hidden, x, gain, out, mixed):
    row, col = place[0], place[2]
    here = lanes(2 * row + col, 256)
    total, line, ffn = own[...], mass[...], own_ffn[...]
    for got in (got1, got2, got3):
        total += got[:256].astype(f32)
        ffn += got[272:528].astype(f32)
        line += got[256:264].astype(f32) + got[264:272].astype(f32)
    scale = norm_scale(x[:256].astype(f32))
    column = turn(line[0:1])
    column = jnp.concatenate([column, column], axis=1)
    v = x[:256, here].astype(f32)
    mixed[...] = (hidden[...] + ffn).astype(low)
    out[...] = (dh[...] + scale * gain[0:1, here] * total - v * (scale * scale) * column / 1024).astype(low)


def deal(place, late, early, settled, *messages):
    row, xl = place[0], place[1]

    def total(block, here):
        parts = [late[m, block, here].astype(f32) for m in range(16)]
        while len(parts) > 1:
            parts = [a + b for a, b in zip(parts[::2], parts[1::2])]
        return parts[0].astype(low)

    for j, message in enumerate(messages):
        r, half = row ^ (j >> 1), xl ^ (j & 1)
        message[0:64] = total(2 * r + half, slice(None))
        for i in range(10):
            message[64 + 16 * i : 80 + 16 * i] = early[pl.ds(pl.multiple_of((10 * r + i) * 32 + 16 * half, 16), 16)]
    settled[0:64] = total(4, slice(None))
    settled[64:384] = early[640:960]


def place_out(place, settled, m0, m1, m2, m3, g_in, g_out, g_gu, g_down, small, cross):
    row, xl, col = place[0], place[1], place[2]
    spot = 2 * row + xl
    got = (m0, m1, m2, m3)

    def sender(q, here):
        return jnp.where(
            spot == q,
            got[0][here],
            jnp.where(spot == (q ^ 1), got[1][here], jnp.where(spot == (q ^ 2), got[2][here], got[3][here])),
        ).astype(f32)

    extra = jnp.zeros((16, 128), f32)
    for q in range(4):
        whole = sender(q, slice(None))
        for k in range(3):
            g_in[k, :, 128 * q : 128 * q + 128] = whole[16 * k : 16 * k + 16]
        extra += whole[48:64]
        first = 9 * q // 2
        for k in (0, 1):
            for t in range(5):
                at = 64 + 16 * (5 * k + t)
                here = slice(128 * (first + t), 128 * (first + t) + 128)
                if q % 2 and t == 0:
                    g_gu[:, k, here] += whole[at : at + 16]
                else:
                    g_gu[:, k, here] = whole[at : at + 16]
    swap = col == 1
    small[...] = jnp.concatenate([jnp.where(swap, extra[2:4], extra[0:2]), extra[4:]], axis=0)
    cross[...] = jnp.concatenate([jnp.where(swap, extra[0:2], extra[2:4]), extra[:6]], axis=0)
    for t in range(4):
        here = slice(128 * t, 128 * t + 128)
        g_out[:, here] = settled[16 * t : 16 * t + 16].astype(f32)
        g_down[:, here] = settled[64 + 80 * t : 144 + 80 * t].astype(f32)[:72]


def local(
    tokens,
    segment_ids,
    gain_one,
    in_weight,
    conv_weight,
    out_weight,
    gain_two,
    gate_up,
    down_weight,
    cotangent,
):
    yy, xl, zz, row, col = (lax.axis_index(a) for a in AXES)
    q = 2 * row + xl
    place = jnp.stack([row, xl, col, yy, zz]).astype(jnp.int32)

    def cut(value, index, size, axis):
        return lax.dynamic_slice_in_dim(value, index * size, size, axis)

    def window(value, index, axis):
        return lax.dynamic_slice_in_dim(value, (9 * index // 2) * 128, 640, axis)

    extra = []
    for gain in (gain_one, gain_two):
        for _ in range(3):
            piece = lax.reduce_precision(gain, 8, 7)
            extra.append(piece)
            gain = gain - piece
    extra.append(segment_ids.astype(f32))
    extra = jnp.pad(jnp.stack(extra), ((0, 9), (0, 0))).astype(low)
    piece = jnp.concatenate([tokens, extra])
    in_w = in_weight.transpose(1, 0, 2)
    in_own, in_send = cut(in_w, q, 128, 2), cut(in_w, 3 - q, 128, 2)
    in_send = jnp.concatenate([in_send[:, :256], in_send[:, 256:]], axis=2).reshape(768, 256)
    near = [piece, ring(piece, 1), ring(piece, 2), ring(jnp.concatenate([piece, in_send]), 3)]
    taps = jnp.pad(cut(conv_weight, xl, 128, 0).T.astype(f32), ((0, 5), (0, 0)))

    def begin(index):
        return (9 * index // 2) * 128

    m = 4 * yy + zz
    gu_part = lax.dynamic_slice(gate_up, (32 * m, 0, begin(3 - q)), (32, 2, 640))
    gu_part = gu_part.reshape(32, 2, 5, 128).transpose(1, 2, 0, 3).reshape(320, 128)
    down_part = lax.dynamic_slice(down_weight, (begin(3 - q) + 16 * (5 * m // 2), 0), (48, 512))
    down_part = down_part.reshape(48, 4, 128).transpose(1, 0, 2).reshape(192, 128)
    out_part = cut(out_weight, m, 32, 0).reshape(32, 4, 128).transpose(1, 0, 2).reshape(128, 128)
    pack = ring(jnp.concatenate([gu_part, down_part, out_part]), 3)
    cross = moved(out_part, ("xl", "row", "col"), lambda xl, row, col: (1 - xl, 1 - row, 1 - col))
    packs = lax.all_gather(jnp.concatenate([pack, cross]), ("y", "z"))
    out_swap = swap_core(out_weight)
    gu_own, down_own = window(gate_up.transpose(1, 0, 2), q, 2), window(down_weight, q, 0)

    out_line = cut(out_weight, q, 128, 0)
    in_own, gu_own, down_own, taps, out_line, place, near[1] = lax.optimization_barrier(
        (in_own, gu_own, down_own, taps, out_line, place, near[1])
    )
    far = [swap_core(v) for v in near[:3]] + [swap_core(near[3][:272])]
    tile = shaped(512, 128)
    tile_low = shaped(512, 128, kind=low)
    whole_low = shaped(512, 1024, kind=low)
    x, n_one, gain, b, c, u, bx, tails, tail, same_one, same_two, scale = call(
        front,
        [
            whole_low,
            whole_low,
            shaped(16, 1024),
            tile,
            tile,
            tile,
            tile_low,
            shaped(2, 8, 128),
            shaped(8, 128),
            tile,
            tile,
            tile,
        ],
        [pltpu.VMEM((3, 512, 128), low)],
        place,
        *near,
        *far,
        in_own,
    )
    in_far = near[3][272:].reshape(3, 256, 2, 128).transpose(0, 2, 1, 3).reshape(3, 512, 128)
    df, tails = lax.optimization_barrier((cotangent, tails))
    df_near = [df] + [ring(df, k) for k in (1, 2, 3)]
    df_far = [swap_core(v) for v in df_near]
    prior = moved(tails, ("z",), lambda z: ((z + 1) % 4,))
    first = moved(tail, ("y", "z"), lambda y, z: (y + 1, 0) if z == 3 and y < 3 else None)
    conv, y, y_swap, past_one, past_two = call(
        conv_forward, [tile, tile_low, tile_low, tile, tile], [], place, bx, prior, first, c, same_one, same_two, taps
    )
    near = [y, ring(y_swap, 1), ring(y, 2), ring(y_swap, 3)]
    far = [swap_core(v) for v in near]

    hid_low = shaped(512, 640, kind=low)
    keep4, send4 = shaped(4, 256, 256), shaped(4, 256, 256, kind=low)
    send4_mass = shaped(4, 272, 256, kind=low)
    hidden, n_two, act, dgate, dup, keep, send, df, down_far, out_row = call(
        feed,
        [
            shaped(512, 1024),
            whole_low,
            hid_low,
            hid_low,
            hid_low,
            keep4,
            send4,
            whole_low,
            shaped(640, 512, kind=low),
            shaped(128, 512, kind=low),
        ],
        [
            pltpu.VMEM((512, 1024), low),
            pltpu.VMEM((512, 1024), f32),
            pltpu.VMEM((512, 640), f32),
            pltpu.VMEM((512, 640), f32),
            pltpu.VMEM((512, 640), f32),
            pltpu.VMEM((2, 512, 640), low),
            pltpu.VMEM((1024, 512), low),
        ],
        place,
        *near,
        *far,
        x,
        gain,
        out_weight,
        out_swap,
        gu_own,
        down_own,
        *df_near,
        *df_far,
        packs,
    )
    got = swap_core(send)
    own = shaped(256, 256)
    own_low = shaped(256, 256, kind=low)
    dn_own, *parts = call(fold, [own, own_low, own_low, own_low], [], place, keep, got)
    ringed = [ring(v, k) for k, v in zip((1, 2, 3), parts)]
    (early,) = call(
        feed_weights,
        [shaped(16, 960, 128, kind=low)],
        [pltpu.VMEM((640, 1024), f32)],
        place,
        n_two,
        act,
        dgate,
        dup,
        df,
    )
    dn_own, early = lax.optimization_barrier((dn_own, early))
    early = early.reshape(16 * 960, 128)
    early = lax.psum_scatter(early, ("y", "z"), scatter_dimension=0, tiled=True)
    piece = (dn_own + sum(v.astype(f32) for v in ringed)).astype(low)
    near = [piece] + [ring(piece, k) for k in (1, 2, 3)]
    far = [swap_core(v) for v in near]
    dh_own, do, dconv, dc, heads, head, dg_two = call(
        mix_backward,
        [own, whole_low, tile, tile, shaped(2, 16, 128), shaped(16, 128), shaped(8, 256)],
        [pltpu.VMEM((512, 1024), low)],
        place,
        *near,
        *far,
        hidden,
        df,
        gain,
        out_line,
        out_row,
        c,
        conv,
        same_one,
        same_two,
    )
    act, heads = lax.optimization_barrier((act, heads))
    keep_ffn, send_ffn = call(
        feed_out, [keep4, send4], [pltpu.VMEM((512, 1024), f32)], place, act, down_own, down_far
    )
    dconv, send_ffn = lax.optimization_barrier((dconv, send_ffn))
    got_ffn = swap_core(send_ffn)
    later = moved(heads, ("z",), lambda z: ((z - 1) % 4,))
    last = moved(head, ("y", "z"), lambda y, z: (y - 1, 3) if z == 0 and y > 0 else None)
    dproj, keep, send, total, small = call(
        conv_backward,
        [shaped(512, 384, kind=low), keep4, send4_mass, shaped(2, 8, 256), shaped(2, 16, 128, kind=low)],
        [pltpu.VMEM((512, 1024), f32)],
        place,
        dconv,
        dc,
        later,
        last,
        same_one,
        same_two,
        taps,
        b,
        c,
        u,
        past_one,
        past_two,
        bx,
        in_own,
        in_far,
        x,
        scale,
        dg_two,
    )
    got = swap_core(send)
    own_mass = shaped(528, 256, kind=low)
    dn_own, ffn_own, mass, *parts = call(
        fold_last,
        [own, own, shaped(8, 256), own_mass, own_mass, own_mass],
        [],
        place,
        keep,
        got,
        keep_ffn,
        got_ffn,
        total,
    )
    (late,) = call(mix_weights, [shaped(16, 5, 64, 128, kind=low)], [], place, n_one, dproj, y, do, small)
    ringed = [ring(v, k) for k, v in zip((1, 2, 3), parts)]
    late = lax.all_to_all(late, ("y", "z"), 0, 0)
    h_own = lax.dynamic_slice_in_dim(hidden[:256], (2 * row + col) * 256, 256, 1)
    grad_tokens, mixed = call(
        finish, [own_low, own_low], [], place, dn_own, ffn_own, mass, *ringed, dh_own, h_own, x, gain
    )

    late, grad_tokens, mixed = lax.optimization_barrier((late, grad_tokens, mixed))

    settled, *messages = call(
        deal, [shaped(384, 128, kind=low)] + [shaped(224, 128, kind=low)] * 4, [], place, late, early
    )
    settled = moved(
        settled, ("y", "xl", "z", "row"), lambda y, xl, z, r: (2 * r + xl, y % 2, z, y // 2)
    )
    messages = [messages[0]] + [ring(messages[k], k) for k in (1, 2, 3)]
    grad_in, grad_out, grad_gate_up, grad_down, small, cross = call(
        place_out,
        [
            shaped(3, 16, 512),
            shaped(16, 512),
            shaped(16, 2, 2304),
            shaped(72, 512),
            shaped(14, 128),
            shaped(8, 128),
        ],
        [],
        place,
        settled,
        *messages,
    )
    cross = swap_core(cross)
    small = jnp.concatenate([small[:2] + cross[:2], small[2:10]]).reshape(5, 256)
    small = cut(small, 8 * yy + 4 * xl + zz, 8, 1)
    return (
        mixed,
        grad_tokens,
        small[0],
        grad_in.transpose(1, 0, 2),
        small[2:5].T,
        grad_out,
        small[1],
        grad_gate_up,
        grad_down,
    )


def solution(mesh):
    dp = ("y", "xl", "z")
    fine = Mesh(mesh.devices.reshape(tuple(SIZES.values())), AXES)
    return jax.shard_map(
        local,
        mesh=fine,
        in_specs=(
            P(dp, ("row", "col")),
            P(dp),
            P(("row", "col")),
            P("row", None, "col"),
            P(("col", "row"), None),
            P("col", "row"),
            P(("row", "col")),
            P("row", None, "col"),
            P("col", "row"),
            P(dp, ("row", "col")),
        ),
        out_specs=(
            P(dp, ("row", "col")),
            P(dp, ("row", "col")),
            P(("row", "col", *dp)),
            P(("row", *dp), None, "col"),
            P(("col", "row", *dp), None),
            P(("col", *dp), "row"),
            P(("row", "col", *dp)),
            P(("row", *dp), None, "col"),
            P(("col", *dp), "row"),
        ),
        check_vma=False,
    )
```

```python
import functools

import jax
import jax.numpy as jnp
from jax import lax
from jax.experimental import pallas as pl
from jax.experimental.pallas import tpu as pltpu
from jax.sharding import Mesh, PartitionSpec as P

eps_norm = 1e-05
f32 = jnp.float32
low = jnp.bfloat16
SIZES = {"y": 4, "xl": 2, "z": 4, "row": 2, "col": 2}
AXES = tuple(SIZES)


def moved(value, axes, place):
    sizes = [SIZES[a] for a in axes]
    pairs = []
    count = 1
    for size in sizes:
        count *= size
    for source in range(count):
        rest, coords = source, []
        for size in reversed(sizes):
            coords.insert(0, rest % size)
            rest //= size
        target = place(*coords)
        if target is None:
            continue
        index = 0
        for size, at in zip(sizes, target):
            index = index * size + at
        pairs.append((source, index))
    return lax.ppermute(value, axes if len(axes) > 1 else axes[0], pairs)


def ring(value, k):
    return moved(value, ("xl", "row"), lambda xl, row: (xl ^ (k & 1), row ^ (k >> 1)))


def swap_core(value):
    return moved(value, ("col",), lambda col: (1 - col,))


def by_core(col, near, far):
    first = col == 0
    return jnp.where(first, near, far), jnp.where(first, far, near)


def dot(a, b, dims):
    return lax.dot_general(a, b, (dims, ((), ())), preferred_element_type=f32)


def mm(a, b):
    return dot(a, b, ((1,), (0,)))


def mm_t(a, b):
    return dot(a, b, ((1,), (1,)))


def lanes(index, size):
    return pl.ds(pl.multiple_of(index * size, size), size)


def rows(index, size):
    return pl.ds(pl.multiple_of(index * size, size), size)


def shaped(*shape, kind=f32):
    return jax.ShapeDtypeStruct(shape, kind)


def call(body, outs, scratch, place, *args):
    spec = pl.BlockSpec(memory_space=pltpu.VMEM)
    return pl.pallas_call(
        body,
        out_shape=outs,
        in_specs=[pl.BlockSpec(memory_space=pltpu.SMEM)] + [spec] * len(args),
        out_specs=[spec] * len(outs),
        scratch_shapes=scratch,
        compiler_params=pltpu.CompilerParams(vmem_limit_bytes=56 * 2**20),
    )(place, *args)


def turn(row):
    return jnp.broadcast_to(row, (128, 256)).T


def assemble(out, row, col, near, far):
    for k in range(4):
        at = (row ^ (k >> 1)) * 2
        here = slice((k & 1) * 256, (k & 1) * 256 + 256)
        out[here, lanes(at + col, 256)] = near[k][:256]
        out[here, lanes(at + 1 - col, 256)] = far[k][:256]


def norm_scale(value):
    return lax.rsqrt(jnp.sum(value * value, axis=1, keepdims=True) / 1024 + eps_norm)


def front(place, *refs):
    near, far, w_own = refs[0:4], refs[4:8], refs[8]
    x, n, gain, b, c, u, bx, tails, tail, same_one, same_two, scale, w_far = refs[9:]
    row, xl, col = place[0], place[1], place[2]
    assemble(x, row, col, near, far)
    for k in (0, 2):
        for piece, at in ((near[k], col), (far[k], 1 - col)):
            extra = piece[256:272].astype(f32)
            for i in (0, 1):
                total = extra[3 * i : 3 * i + 1] + extra[3 * i + 1 : 3 * i + 2] + extra[3 * i + 2 : 3 * i + 3]
                gain[8 * i : 8 * i + 8, lanes((row ^ (k >> 1)) * 2 + at, 256)] = jnp.broadcast_to(total, (8, 256))
    for i in (0, 1):
        ids = turn(near[i][256:272].astype(f32)[6:7])
        one = jnp.concatenate([ids[:1], ids[:-1]])
        two = jnp.concatenate([ids[:1], ids[:1], ids[:-2]])
        same_one[256 * i : 256 * i + 256] = jnp.where(ids == one, 1.0, 0.0)
        same_two[256 * i : 256 * i + 256] = jnp.where(ids == two, 1.0, 0.0)

    @pl.loop(0, 8)
    def _(i):
        v = x[rows(i, 64)].astype(f32)
        r = norm_scale(v)
        scale[rows(i, 64)] = jnp.broadcast_to(r, (64, 128))
        n[rows(i, 64)] = (v * r * gain[0:1]).astype(low)

    for i in range(3):
        for e in (0, 1):
            w_far[i, 256 * e : 256 * e + 256] = near[3][272 + 256 * i : 528 + 256 * i, 128 * e : 128 * e + 128]
    n_own, n_far = n[:, lanes(row, 512)], n[:, lanes(1 - row, 512)]
    for i, out in enumerate((b, c, u)):
        out[...] = mm(n_own, w_own[i]) + mm(n_far, w_far[i])
    bx[...] = (b[...] * u[...]).astype(low)
    ends = bx[240:256].astype(f32)[8:], bx[496:512].astype(f32)[8:]
    first = xl == 0
    tails[0] = jnp.where(first, ends[0], ends[1])
    tails[1] = jnp.where(first, ends[1], ends[0])
    tail[...] = jnp.where(first, ends[1], ends[0])


def conv_forward(place, bx, prior, first, c, same_one, same_two, taps, conv, y, y_swap, past_one, past_two):
    xl, zz = place[1], place[4]
    start = zz == 0
    rim = jnp.where(start, first[...], prior[0]), jnp.where(start, prior[0], prior[1])
    for i in (0, 1):
        here = slice(256 * i, 256 * i + 256)
        there = slice(256 - 256 * i, 512 - 256 * i)
        v = bx[here].astype(f32)
        ext = jnp.concatenate([jnp.where(xl == i, rim[0], rim[1]), v])
        one = ext[7:263] * same_one[here]
        two = ext[6:262] * same_two[here]
        past_one[here] = one
        past_two[here] = two
        total = taps[2:3] * v + taps[1:2] * one + taps[0:1] * two
        conv[here] = total
        mixed = (c[here] * total).astype(low)
        y[here] = mixed
        y_swap[there] = mixed


def feed(place, *refs):
    near, far = refs[0:4], refs[4:8]
    x, gain, out_own, out_swap, gu_own, down_own = refs[8:14]
    df_near, df_far, packs = refs[14:18], refs[18:22], refs[22]
    hidden, n, act, dgate, dup, keep, send, df, down_far, out_row = refs[23:33]
    y, wide, gate, up, dact, gu_far, out_far = refs[33:]
    row, xl, col = place[0], place[1], place[2]
    q = 2 * row + xl
    for m in range(16):
        for k in (0, 1):
            for t in range(5):
                at = (5 * k + t) * 32
                gu_far[k, 32 * m : 32 * m + 32, 128 * t : 128 * t + 128] = packs[m, at : at + 32]
        for t in range(4):
            first = 16 * (5 * m // 2)
            at = 320 + 48 * t
            down_far[first : first + 48, 128 * t : 128 * t + 128] = packs[m, at : at + 48]
            for e in (0, 1):
                at = 512 + (4 * e + t) * 32
                out_far[512 * e + 32 * m : 512 * e + 32 * m + 32, 128 * t : 128 * t + 128] = packs[m, at : at + 32]
    out_row[...] = out_far[rows(q, 128)]
    for k in range(4):
        y[:, lanes(col * 4 + (q ^ k), 128)] = near[k][...]
        y[:, lanes((1 - col) * 4 + (q ^ k), 128)] = far[k][...]
    assemble(df, row, col, df_near, df_far)
    y_own, y_far = y[:, lanes(col, 512)], y[:, lanes(1 - col, 512)]
    wide[:, lanes(row, 512)] = mm(y_own, out_own[...]) + mm(y_far, out_swap[...])
    wide[:, lanes(1 - row, 512)] = mm(y_own, out_far[:512]) + mm(y_far, out_far[512:])

    @pl.loop(0, 8)
    def _(i):
        h = x[rows(i, 64)].astype(f32) + wide[rows(i, 64)]
        hidden[rows(i, 64)] = h
        n[rows(i, 64)] = (h * norm_scale(h) * gain[8:9]).astype(low)

    n_own, n_far = n[:, lanes(row, 512)], n[:, lanes(1 - row, 512)]
    gate[...] = mm(n_own, gu_own[0]) + mm(n_far, gu_far[0])
    up[...] = mm(n_own, gu_own[1]) + mm(n_far, gu_far[1])
    dact[...] = mm_t(df[:, lanes(row, 512)], down_own[...]) + mm_t(df[:, lanes(1 - row, 512)], down_far[...])
    lane = lax.broadcasted_iota(jnp.int32, (64, 640), 1) - 64 * xl
    mine = (lane >= 0) & (lane < 576)

    @pl.loop(0, 8)
    def _(i):
        at = rows(i, 64)
        g = jnp.where(mine, gate[at], 0.0)
        v = jnp.where(mine, up[at], 0.0)
        da = dact[at]
        s = 1.0 / (1.0 + jnp.exp(-g))
        gs = g * s
        act[at] = (gs * v).astype(low)
        dgate[at] = (da * v * s * (1.0 + g * (1.0 - s))).astype(low)
        dup[at] = (da * gs).astype(low)

    for k, w in ((0, gu_own), (1, gu_far)):
        wide[:, 512 * k : 512 * k + 512] = mm_t(dgate[...], w[0]) + mm_t(dup[...], w[1])
    part(wide, keep, send, col)


def part(wide, keep, send, col):
    for k in range(4):
        here = slice(256 * (k & 1), 256 * (k & 1) + 256)
        keep[k] = wide[here, lanes(2 * (k >> 1) + col, 256)]
        send[k, :256] = wide[here, lanes(2 * (k >> 1) + 1 - col, 256)].astype(low)


def feed_out(place, act, down_own, down_far, keep, send, wide):
    for k, w in ((0, down_own), (1, down_far)):
        wide[:, 512 * k : 512 * k + 512] = mm(act[...], w[...])
    part(wide, keep, send, place[2])


def source_row(m, half):
    return 128 * (m // 4) + 64 * half + 16 * (m % 4)


def feed_weights(place, n, act, dgate, dup, df, early, wide):
    xl = place[1]
    n_t = n[...].T
    for k, g in ((0, dgate), (1, dup)):
        for r in (0, 1):
            total = mm(n_t[512 * r : 512 * r + 512], g[...]).astype(low)
            for m in range(16):
                for t in range(5):
                    for h in (0, 1):
                        at = ((r * 2 + k) * 5 + t) * 32 + 16 * h
                        first = source_row(m, h)
                        early[m, at : at + 16] = total[first : first + 16, 128 * t : 128 * t + 128]
    wide[...] = mm(act[...].T, df[...])
    for i in range(8):
        some = wide[pl.ds(pl.multiple_of(64 * xl + 72 * i, 8), 72)]
        some = jnp.concatenate([some, jnp.zeros((8, 1024), f32)]).astype(low)
        for r in (0, 1):
            for t in range(4):
                early[8 * r + i, 640 + 80 * t : 720 + 80 * t] = some[:, 512 * r + 128 * t : 512 * r + 128 * t + 128]


def fold(place, keep, got, own, *others):
    own[...] = keep[0] + got[0].astype(f32)
    for k in (1, 2, 3):
        others[k - 1][...] = (keep[k] + got[k].astype(f32)).astype(low)


def mix_backward(place, *refs):
    near, far = refs[0:4], refs[4:8]
    hidden, df, gain, w_own, w_far, c, conv, same_one, same_two = refs[8:17]
    dh_own, do, dconv, dc, heads, head, dg_two = refs[17:24]
    (dn,) = refs[24:]
    row, xl, col = place[0], place[1], place[2]
    assemble(dn, row, col, near, far)
    own = lanes(2 * row + col, 256)
    dg_two[...] = jnp.zeros((8, 256), f32)

    @pl.loop(0, 8)
    def _(i):
        at = rows(i, 64)
        h = hidden[at]
        r = norm_scale(h)
        d = dn[at].astype(f32)
        scaled = d * gain[8:9]
        total = jnp.sum(scaled * h, axis=1, keepdims=True)
        dh = df[at].astype(f32) + r * scaled - h * (r * r * r * total / 1024)
        do[at] = dh.astype(low)

        @pl.when(i < 4)
        def _():
            h = hidden[at, own]
            d = dn[at, own].astype(f32)
            dh_own[at] = df[at, own].astype(f32) + r * d * gain[8:9, own] - h * (r * r * r * total / 1024)
            dg_two[...] += jnp.broadcast_to(jnp.sum(d * h * r, axis=0, keepdims=True), (8, 256))

    dy = mm_t(do[:, lanes(row, 512)], w_own[...]) + mm_t(do[:, lanes(1 - row, 512)], w_far[...])
    edge = dy * c[...]
    dconv[...] = edge
    dc[...] = dy * conv[...]
    ends = [
        jnp.concatenate([edge[at : at + 8] * same_one[at : at + 8], edge[at : at + 8] * same_two[at : at + 8]])
        for at in (0, 256)
    ]
    first = xl == 0
    heads[0] = jnp.where(first, ends[0], ends[1])
    heads[1] = jnp.where(first, ends[1], ends[0])
    head[...] = jnp.where(first, ends[0], ends[1])


def conv_backward(place, *refs):
    dconv, dc, later, last, same_one, same_two, taps, b, c, u, past_one, past_two, bx, w_own, w_far = refs[:15]
    x, scale, dg_two = refs[15:18]
    dproj, keep, send, total, small = refs[18:23]
    (wide,) = refs[23:]
    row, xl, col, zz = place[0], place[1], place[2], place[4]
    end = zz == 3
    rim = jnp.where(end, later[1], later[0]), jnp.where(end, last[...], later[1])
    parts = []
    for i in (0, 1):
        here = slice(256 * i, 256 * i + 256)
        d = dconv[here]
        edge = jnp.where(xl == i, rim[0], rim[1])
        one = jnp.concatenate([d * same_one[here], edge[:8]])
        two = jnp.concatenate([d * same_two[here], edge[8:]])
        dbx = taps[2:3] * d + taps[1:2] * one[1:257] + taps[0:1] * two[2:258]
        parts.append(jnp.concatenate([
            jnp.sum(d * past_two[here], axis=0, keepdims=True),
            jnp.sum(d * past_one[here], axis=0, keepdims=True),
            jnp.sum(d * bx[here].astype(f32), axis=0, keepdims=True),
            jnp.zeros((5, 128), f32),
        ]))
        db = (dbx * u[here]).astype(low)
        dcv = dc[here].astype(low)
        du = (dbx * b[here]).astype(low)
        dproj[here, 0:128] = db
        dproj[here, 128:256] = dcv
        dproj[here, 256:384] = du
        mass = jnp.sum(
            db.astype(f32) * b[here] + dcv.astype(f32) * c[here] + du.astype(f32) * u[here], axis=1, keepdims=True
        )
        line = jnp.broadcast_to(mass, (256, 128)).T[:8]
        total[i] = line
        high = line.astype(low)
        rest = (line - high.astype(f32)).astype(low)
        both = jnp.concatenate([high, rest])
        send[i, 256:272] = both
        send[2 + i, 256:272] = both
    zero = jnp.zeros((1, 128), f32)
    for k, w in ((0, w_own), (1, w_far)):
        whole = jnp.concatenate([w[0], w[1], w[2]], axis=1)
        wide[:, 512 * k : 512 * k + 512] = mm_t(dproj[...], whole)
        sums = jnp.zeros((1, 512), f32)
        for i in range(8):
            here = slice(64 * i, 64 * i + 64)
            v = x[here, lanes(row ^ k, 512)].astype(f32)
            r = scale[here]
            r = jnp.concatenate([r, r, r, r], axis=1)
            sums += jnp.sum(wide[here, 512 * k : 512 * k + 512] * v * r, axis=0, keepdims=True)
        lines = [sums[:, 128 * t : 128 * t + 128] for t in range(4)]
        if k == 0:
            lines += [dg_two[0:1, :128], dg_two[0:1, 128:]]
            for a in range(3):
                tap = parts[0][a : a + 1] + parts[1][a : a + 1]
                lines += [jnp.where(xl == 0, tap, zero), jnp.where(xl == 0, zero, tap)]
        lines += [zero] * (16 - len(lines))
        small[row ^ k] = jnp.concatenate(lines).astype(low)
    part(wide, keep, send, col)


def mix_weights(place, n, dproj, y, do, small, late):
    n_t = n[...].T
    for r in (0, 1):
        total = mm(n_t[512 * r : 512 * r + 512], dproj[...]).astype(low)
        for m in range(16):
            for h in (0, 1):
                for k in range(3):
                    first = source_row(m, h)
                    at = 48 * (2 * r + h) + 16 * k
                    late[m, at : at + 16] = total[first : first + 16, 128 * k : 128 * k + 128]
            late[m, 256 + 16 * r : 272 + 16 * r] = small[r]
    total = mm(y[...].T, do[...]).astype(low)
    for r in (0, 1):
        for i in range(8):
            for t in range(4):
                late[8 * r + i, 192 + 16 * t : 208 + 16 * t] = total[
                    16 * i : 16 * i + 16, 512 * r + 128 * t : 512 * r + 128 * t + 128
                ]


def fold_last(place, keep, got, keep_ffn, got_ffn, total, own, own_ffn, mass, *others):
    for k in range(4):
        whole = keep[k] + got[k, :256].astype(f32)
        line = total[k & 1] + got[k, 256:264].astype(f32) + got[k, 264:272].astype(f32)
        ffn = keep_ffn[k] + got_ffn[k].astype(f32)
        if k == 0:
            own[...] = whole
            own_ffn[...] = ffn
            mass[...] = line
        else:
            others[k - 1][272:528] = ffn.astype(low)
            others[k - 1][:256] = whole.astype(low)
            high = line.astype(low)
            others[k - 1][256:272] = jnp.concatenate([high, (line - high.astype(f32)).astype(low)])


def finish(place, own, own_ffn, mass, got1, got2, got3, dh, hidden, x, gain, out, mixed):
    row, col = place[0], place[2]
    here = lanes(2 * row + col, 256)
    total, line, ffn = own[...], mass[...], own_ffn[...]
    for got in (got1, got2, got3):
        total += got[:256].astype(f32)
        ffn += got[272:528].astype(f32)
        line += got[256:264].astype(f32) + got[264:272].astype(f32)
    scale = norm_scale(x[:256].astype(f32))
    column = turn(line[0:1])
    column = jnp.concatenate([column, column], axis=1)
    v = x[:256, here].astype(f32)
    mixed[...] = (hidden[...] + ffn).astype(low)
    out[...] = (dh[...] + scale * gain[0:1, here] * total - v * (scale * scale) * column / 1024).astype(low)


def deal(place, late, early, settled, *messages):
    row, xl = place[0], place[1]

    def total(here):
        parts = [late[m, here].astype(f32) for m in range(16)]
        while len(parts) > 1:
            parts = [a + b for a, b in zip(parts[::2], parts[1::2])]
        return parts[0].astype(low)

    for j, message in enumerate(messages):
        r, half = row ^ (j >> 1), xl ^ (j & 1)
        message[0:48] = total(pl.ds(pl.multiple_of(48 * (2 * r + half), 16), 48))
        message[48:64] = total(rows(16 + r, 16))
        for i in range(10):
            message[64 + 16 * i : 80 + 16 * i] = early[pl.ds(pl.multiple_of((10 * r + i) * 32 + 16 * half, 16), 16)]
    settled[0:64] = total(slice(192, 256))
    settled[64:384] = early[640:960]


def place_out(place, settled, m0, m1, m2, m3, g_in, g_out, g_gu, g_down):
    spot = 2 * place[0] + place[1]
    got = (m0, m1, m2, m3)

    def sender(q, here):
        return jnp.where(
            spot == q,
            got[0][here],
            jnp.where(spot == (q ^ 1), got[1][here], jnp.where(spot == (q ^ 2), got[2][here], got[3][here])),
        ).astype(f32)

    for q in range(4):
        whole = sender(q, slice(None))
        for k in range(3):
            g_in[k, :, 128 * q : 128 * q + 128] = whole[16 * k : 16 * k + 16]
        first = 9 * q // 2
        for k in (0, 1):
            for t in range(5):
                at = 64 + 16 * (5 * k + t)
                here = slice(128 * (first + t), 128 * (first + t) + 128)
                if q % 2 and t == 0:
                    g_gu[:, k, here] += whole[at : at + 16]
                else:
                    g_gu[:, k, here] = whole[at : at + 16]
    for t in range(4):
        here = slice(128 * t, 128 * t + 128)
        g_out[:, here] = settled[16 * t : 16 * t + 16].astype(f32)
        g_down[:, here] = settled[64 + 80 * t : 144 + 80 * t].astype(f32)[:72]


def local(
    tokens,
    segment_ids,
    gain_one,
    in_weight,
    conv_weight,
    out_weight,
    gain_two,
    gate_up,
    down_weight,
    cotangent,
):
    yy, xl, zz, row, col = (lax.axis_index(a) for a in AXES)
    q = 2 * row + xl
    place = jnp.stack([row, xl, col, yy, zz]).astype(jnp.int32)

    def cut(value, index, size, axis):
        return lax.dynamic_slice_in_dim(value, index * size, size, axis)

    def window(value, index, axis):
        return lax.dynamic_slice_in_dim(value, (9 * index // 2) * 128, 640, axis)

    extra = []
    for gain in (gain_one, gain_two):
        for _ in range(3):
            piece = lax.reduce_precision(gain, 8, 7)
            extra.append(piece)
            gain = gain - piece
    extra.append(segment_ids.astype(f32))
    extra = jnp.pad(jnp.stack(extra), ((0, 9), (0, 0))).astype(low)
    piece = jnp.concatenate([tokens, extra])
    in_w = in_weight.transpose(1, 0, 2)
    in_own, in_send = cut(in_w, q, 128, 2), cut(in_w, 3 - q, 128, 2)
    in_send = jnp.concatenate([in_send[:, :256], in_send[:, 256:]], axis=2).reshape(768, 256)
    near = [piece, ring(piece, 1), ring(piece, 2), ring(jnp.concatenate([piece, in_send]), 3)]
    taps = jnp.pad(cut(conv_weight, xl, 128, 0).T.astype(f32), ((0, 5), (0, 0)))

    def begin(index):
        return (9 * index // 2) * 128

    m = 4 * yy + zz
    gu_part = lax.dynamic_slice(gate_up, (32 * m, 0, begin(3 - q)), (32, 2, 640))
    gu_part = gu_part.reshape(32, 2, 5, 128).transpose(1, 2, 0, 3).reshape(320, 128)
    down_part = lax.dynamic_slice(down_weight, (begin(3 - q) + 16 * (5 * m // 2), 0), (48, 512))
    down_part = down_part.reshape(48, 4, 128).transpose(1, 0, 2).reshape(192, 128)
    out_part = cut(out_weight, m, 32, 0).reshape(32, 4, 128).transpose(1, 0, 2).reshape(128, 128)
    pack = ring(jnp.concatenate([gu_part, down_part, out_part]), 3)
    cross = moved(out_part, ("xl", "row", "col"), lambda xl, row, col: (1 - xl, 1 - row, 1 - col))
    packs = lax.all_gather(jnp.concatenate([pack, cross]), ("y", "z"))
    out_swap = swap_core(out_weight)
    gu_own, down_own = window(gate_up.transpose(1, 0, 2), q, 2), window(down_weight, q, 0)

    out_line = cut(out_weight, q, 128, 0)
    in_own, gu_own, down_own, taps, out_line, place, near[1] = lax.optimization_barrier(
        (in_own, gu_own, down_own, taps, out_line, place, near[1])
    )
    far = [swap_core(v) for v in near[:3]] + [swap_core(near[3][:272])]
    tile = shaped(512, 128)
    tile_low = shaped(512, 128, kind=low)
    whole_low = shaped(512, 1024, kind=low)
    x, n_one, gain, b, c, u, bx, tails, tail, same_one, same_two, scale = call(
        front,
        [
            whole_low,
            whole_low,
            shaped(16, 1024),
            tile,
            tile,
            tile,
            tile_low,
            shaped(2, 8, 128),
            shaped(8, 128),
            tile,
            tile,
            tile,
        ],
        [pltpu.VMEM((3, 512, 128), low)],
        place,
        *near,
        *far,
        in_own,
    )
    in_far = near[3][272:].reshape(3, 256, 2, 128).transpose(0, 2, 1, 3).reshape(3, 512, 128)
    df, tails = lax.optimization_barrier((cotangent, tails))
    df_near = [df] + [ring(df, k) for k in (1, 2, 3)]
    df_far = [swap_core(v) for v in df_near]
    prior = moved(tails, ("z",), lambda z: ((z + 1) % 4,))
    first = moved(tail, ("y", "z"), lambda y, z: (y + 1, 0) if z == 3 and y < 3 else None)
    conv, y, y_swap, past_one, past_two = call(
        conv_forward, [tile, tile_low, tile_low, tile, tile], [], place, bx, prior, first, c, same_one, same_two, taps
    )
    near = [y, ring(y_swap, 1), ring(y, 2), ring(y_swap, 3)]
    far = [swap_core(v) for v in near]

    hid_low = shaped(512, 640, kind=low)
    keep4, send4 = shaped(4, 256, 256), shaped(4, 256, 256, kind=low)
    send4_mass = shaped(4, 272, 256, kind=low)
    hidden, n_two, act, dgate, dup, keep, send, df, down_far, out_row = call(
        feed,
        [
            shaped(512, 1024),
            whole_low,
            hid_low,
            hid_low,
            hid_low,
            keep4,
            send4,
            whole_low,
            shaped(640, 512, kind=low),
            shaped(128, 512, kind=low),
        ],
        [
            pltpu.VMEM((512, 1024), low),
            pltpu.VMEM((512, 1024), f32),
            pltpu.VMEM((512, 640), f32),
            pltpu.VMEM((512, 640), f32),
            pltpu.VMEM((512, 640), f32),
            pltpu.VMEM((2, 512, 640), low),
            pltpu.VMEM((1024, 512), low),
        ],
        place,
        *near,
        *far,
        x,
        gain,
        out_weight,
        out_swap,
        gu_own,
        down_own,
        *df_near,
        *df_far,
        packs,
    )
    got = swap_core(send)
    own = shaped(256, 256)
    own_low = shaped(256, 256, kind=low)
    dn_own, *parts = call(fold, [own, own_low, own_low, own_low], [], place, keep, got)
    ringed = [ring(v, k) for k, v in zip((1, 2, 3), parts)]
    (early,) = call(
        feed_weights,
        [shaped(16, 960, 128, kind=low)],
        [pltpu.VMEM((640, 1024), f32)],
        place,
        n_two,
        act,
        dgate,
        dup,
        df,
    )
    dn_own, early = lax.optimization_barrier((dn_own, early))
    early = early.reshape(16 * 960, 128)
    early = lax.psum_scatter(early, ("y", "z"), scatter_dimension=0, tiled=True)
    piece = (dn_own + sum(v.astype(f32) for v in ringed)).astype(low)
    near = [piece] + [ring(piece, k) for k in (1, 2, 3)]
    far = [swap_core(v) for v in near]
    dh_own, do, dconv, dc, heads, head, dg_two = call(
        mix_backward,
        [own, whole_low, tile, tile, shaped(2, 16, 128), shaped(16, 128), shaped(8, 256)],
        [pltpu.VMEM((512, 1024), low)],
        place,
        *near,
        *far,
        hidden,
        df,
        gain,
        out_line,
        out_row,
        c,
        conv,
        same_one,
        same_two,
    )
    act, heads = lax.optimization_barrier((act, heads))
    keep_ffn, send_ffn = call(
        feed_out, [keep4, send4], [pltpu.VMEM((512, 1024), f32)], place, act, down_own, down_far
    )
    dconv, send_ffn = lax.optimization_barrier((dconv, send_ffn))
    got_ffn = swap_core(send_ffn)
    later = moved(heads, ("z",), lambda z: ((z - 1) % 4,))
    last = moved(head, ("y", "z"), lambda y, z: (y - 1, 3) if z == 0 and y > 0 else None)
    dproj, keep, send, total, small = call(
        conv_backward,
        [shaped(512, 384, kind=low), keep4, send4_mass, shaped(2, 8, 256), shaped(2, 16, 128, kind=low)],
        [pltpu.VMEM((512, 1024), f32)],
        place,
        dconv,
        dc,
        later,
        last,
        same_one,
        same_two,
        taps,
        b,
        c,
        u,
        past_one,
        past_two,
        bx,
        in_own,
        in_far,
        x,
        scale,
        dg_two,
    )
    got = swap_core(send)
    own_mass = shaped(528, 256, kind=low)
    dn_own, ffn_own, mass, *parts = call(
        fold_last,
        [own, own, shaped(8, 256), own_mass, own_mass, own_mass],
        [],
        place,
        keep,
        got,
        keep_ffn,
        got_ffn,
        total,
    )
    (late,) = call(mix_weights, [shaped(16, 288, 128, kind=low)], [], place, n_one, dproj, y, do, small)
    ringed = [ring(v, k) for k, v in zip((1, 2, 3), parts)]
    late = lax.all_to_all(late, ("y", "z"), 0, 0)
    h_own = lax.dynamic_slice_in_dim(hidden[:256], (2 * row + col) * 256, 256, 1)
    grad_tokens, mixed = call(
        finish, [own_low, own_low], [], place, dn_own, ffn_own, mass, *ringed, dh_own, h_own, x, gain
    )

    late, grad_tokens, mixed = lax.optimization_barrier((late, grad_tokens, mixed))

    settled, *messages = call(
        deal, [shaped(384, 128, kind=low)] + [shaped(224, 128, kind=low)] * 4, [], place, late, early
    )
    settled = moved(
        settled, ("y", "xl", "z", "row"), lambda y, xl, z, r: (2 * r + xl, y % 2, z, y // 2)
    )
    messages = [messages[0]] + [ring(messages[k], k) for k in (1, 2, 3)]
    extra = sum(message[48:64].astype(f32) for message in messages)
    mine, cross = by_core(col, extra[0:2], extra[2:4])
    cross, settled = lax.optimization_barrier((cross, settled))
    cross = swap_core(cross)
    grad_in, grad_out, grad_gate_up, grad_down = call(
        place_out,
        [shaped(3, 16, 512), shaped(16, 512), shaped(16, 2, 2304), shaped(72, 512)],
        [],
        place,
        settled,
        *messages,
    )
    small = jnp.concatenate([mine + cross, extra[4:12]]).reshape(5, 256)
    small = cut(small, 8 * yy + 4 * xl + zz, 8, 1)
    return (
        mixed,
        grad_tokens,
        small[0],
        grad_in.transpose(1, 0, 2),
        small[2:5].T,
        grad_out,
        small[1],
        grad_gate_up,
        grad_down,
    )


def solution(mesh):
    dp = ("y", "xl", "z")
    fine = Mesh(mesh.devices.reshape(tuple(SIZES.values())), AXES)
    return jax.shard_map(
        local,
        mesh=fine,
        in_specs=(
            P(dp, ("row", "col")),
            P(dp),
            P(("row", "col")),
            P("row", None, "col"),
            P(("col", "row"), None),
            P("col", "row"),
            P(("row", "col")),
            P("row", None, "col"),
            P("col", "row"),
            P(dp, ("row", "col")),
        ),
        out_specs=(
            P(dp, ("row", "col")),
            P(dp, ("row", "col")),
            P(("row", "col", *dp)),
            P(("row", *dp), None, "col"),
            P(("col", "row", *dp), None),
            P(("col", *dp), "row"),
            P(("row", "col", *dp)),
            P(("row", *dp), None, "col"),
            P(("col", *dp), "row"),
        ),
        check_vma=False,
    )
```

```python
import functools

import jax
import jax.numpy as jnp
from jax import lax
from jax.experimental import pallas as pl
from jax.experimental.pallas import tpu as pltpu
from jax.sharding import Mesh, PartitionSpec as P

eps_norm = 1e-05
f32 = jnp.float32
low = jnp.bfloat16
SIZES = {"y": 4, "xl": 2, "z": 4, "row": 2, "col": 2}
AXES = tuple(SIZES)


def moved(value, axes, place):
    sizes = [SIZES[a] for a in axes]
    pairs = []
    count = 1
    for size in sizes:
        count *= size
    for source in range(count):
        rest, coords = source, []
        for size in reversed(sizes):
            coords.insert(0, rest % size)
            rest //= size
        target = place(*coords)
        if target is None:
            continue
        index = 0
        for size, at in zip(sizes, target):
            index = index * size + at
        pairs.append((source, index))
    return lax.ppermute(value, axes if len(axes) > 1 else axes[0], pairs)


def ring(value, k):
    return moved(value, ("xl", "row"), lambda xl, row: (xl ^ (k & 1), row ^ (k >> 1)))


def swap_core(value):
    return moved(value, ("col",), lambda col: (1 - col,))


def by_core(col, near, far):
    first = col == 0
    return jnp.where(first, near, far), jnp.where(first, far, near)


def dot(a, b, dims):
    return lax.dot_general(a, b, (dims, ((), ())), preferred_element_type=f32)


def mm(a, b):
    return dot(a, b, ((1,), (0,)))


def mm_t(a, b):
    return dot(a, b, ((1,), (1,)))


def lanes(index, size):
    return pl.ds(pl.multiple_of(index * size, size), size)


def rows(index, size):
    return pl.ds(pl.multiple_of(index * size, size), size)


def shaped(*shape, kind=f32):
    return jax.ShapeDtypeStruct(shape, kind)


def call(body, outs, scratch, place, *args, loose_in=(), loose_out=()):
    spec, loose = pl.BlockSpec(memory_space=pltpu.VMEM), pl.BlockSpec(memory_space=pl.ANY)
    return pl.pallas_call(
        body,
        out_shape=outs,
        in_specs=[pl.BlockSpec(memory_space=pltpu.SMEM)]
        + [loose if i in loose_in else spec for i in range(len(args))],
        out_specs=[loose if i in loose_out else spec for i in range(len(outs))],
        scratch_shapes=scratch,
        compiler_params=pltpu.CompilerParams(vmem_limit_bytes=56 * 2**20),
    )(place, *args)


def turn(row):
    return jnp.broadcast_to(row, (128, 256)).T


def assemble(out, row, col, near, far):
    for k in range(4):
        at = (row ^ (k >> 1)) * 2
        here = slice((k & 1) * 256, (k & 1) * 256 + 256)
        out[here, lanes(at + col, 256)] = near[k][:256]
        out[here, lanes(at + 1 - col, 256)] = far[k][:256]


def norm_scale(value):
    return lax.rsqrt(jnp.sum(value * value, axis=1, keepdims=True) / 1024 + eps_norm)


def front(place, *refs):
    near, far, w_own = refs[0:4], refs[4:8], refs[8]
    x, n, gain, b, c, u, bx, tails, tail, same_one, same_two, scale, w_far = refs[9:]
    row, xl, col = place[0], place[1], place[2]
    assemble(x, row, col, near, far)
    for k in (0, 2):
        for piece, at in ((near[k], col), (far[k], 1 - col)):
            extra = piece[256:272].astype(f32)
            for i in (0, 1):
                total = extra[3 * i : 3 * i + 1] + extra[3 * i + 1 : 3 * i + 2] + extra[3 * i + 2 : 3 * i + 3]
                gain[8 * i : 8 * i + 8, lanes((row ^ (k >> 1)) * 2 + at, 256)] = jnp.broadcast_to(total, (8, 256))
    for i in (0, 1):
        ids = turn(near[i][256:272].astype(f32)[6:7])
        one = jnp.concatenate([ids[:1], ids[:-1]])
        two = jnp.concatenate([ids[:1], ids[:1], ids[:-2]])
        same_one[256 * i : 256 * i + 256] = jnp.where(ids == one, 1.0, 0.0)
        same_two[256 * i : 256 * i + 256] = jnp.where(ids == two, 1.0, 0.0)

    @pl.loop(0, 8)
    def _(i):
        v = x[rows(i, 64)].astype(f32)
        r = norm_scale(v)
        scale[rows(i, 64)] = jnp.broadcast_to(r, (64, 128))
        n[rows(i, 64)] = (v * r * gain[0:1]).astype(low)

    for i in range(3):
        for e in (0, 1):
            w_far[i, 256 * e : 256 * e + 256] = near[3][272 + 256 * i : 528 + 256 * i, 128 * e : 128 * e + 128]
    n_own, n_far = n[:, lanes(row, 512)], n[:, lanes(1 - row, 512)]
    for i, out in enumerate((b, c, u)):
        out[...] = mm(n_own, w_own[i]) + mm(n_far, w_far[i])
    bx[...] = (b[...] * u[...]).astype(low)
    ends = bx[240:256].astype(f32)[8:], bx[496:512].astype(f32)[8:]
    first = xl == 0
    tails[0] = jnp.where(first, ends[0], ends[1])
    tails[1] = jnp.where(first, ends[1], ends[0])
    tail[...] = jnp.where(first, ends[1], ends[0])


def conv_forward(place, bx, prior, first, c, same_one, same_two, taps, conv, y, y_swap, past_one, past_two):
    xl, zz = place[1], place[4]
    start = zz == 0
    rim = jnp.where(start, first[...], prior[0]), jnp.where(start, prior[0], prior[1])
    for i in (0, 1):
        here = slice(256 * i, 256 * i + 256)
        there = slice(256 - 256 * i, 512 - 256 * i)
        v = bx[here].astype(f32)
        ext = jnp.concatenate([jnp.where(xl == i, rim[0], rim[1]), v])
        one = ext[7:263] * same_one[here]
        two = ext[6:262] * same_two[here]
        past_one[here] = one
        past_two[here] = two
        total = taps[2:3] * v + taps[1:2] * one + taps[0:1] * two
        conv[here] = total
        mixed = (c[here] * total).astype(low)
        y[here] = mixed
        y_swap[there] = mixed


def feed(place, *refs):
    near, far = refs[0:4], refs[4:8]
    x_in, gain, out_own, out_swap, gu_in, down_in = refs[8:14]
    df_near, df_far, packs = refs[14:18], refs[18:22], refs[22]
    hidden_out, n_out, act, dgate, dup, keep, send, df_out, down_out, out_row = refs[23:33]
    y, wide, gate, up, dact, gu_far, out_far, x, gu_own, down_own, hidden, n, df, down_far, sems = refs[33:]
    ins = [
        pltpu.make_async_copy(a, b, sems.at[i])
        for i, (a, b) in enumerate(((x_in, x), (gu_in, gu_own), (down_in, down_own)))
    ]
    outs = [
        pltpu.make_async_copy(a, b, sems.at[3 + i])
        for i, (a, b) in enumerate(((df, df_out), (down_far, down_out), (hidden, hidden_out), (n, n_out)))
    ]
    for copy in ins:
        copy.start()
    row, xl, col = place[0], place[1], place[2]
    q = 2 * row + xl
    for m in range(16):
        for k in (0, 1):
            for t in range(5):
                at = (5 * k + t) * 32
                gu_far[k, 32 * m : 32 * m + 32, 128 * t : 128 * t + 128] = packs[m, at : at + 32]
        for t in range(4):
            first = 16 * (5 * m // 2)
            at = 320 + 48 * t
            down_far[first : first + 48, 128 * t : 128 * t + 128] = packs[m, at : at + 48]
            for e in (0, 1):
                at = 512 + (4 * e + t) * 32
                out_far[512 * e + 32 * m : 512 * e + 32 * m + 32, 128 * t : 128 * t + 128] = packs[m, at : at + 32]
    out_row[...] = out_far[rows(q, 128)]
    for k in range(4):
        y[:, lanes(col * 4 + (q ^ k), 128)] = near[k][...]
        y[:, lanes((1 - col) * 4 + (q ^ k), 128)] = far[k][...]
    assemble(df, row, col, df_near, df_far)
    outs[0].start()
    outs[1].start()
    y_own, y_far = y[:, lanes(col, 512)], y[:, lanes(1 - col, 512)]
    wide[:, lanes(row, 512)] = mm(y_own, out_own[...]) + mm(y_far, out_swap[...])
    wide[:, lanes(1 - row, 512)] = mm(y_own, out_far[:512]) + mm(y_far, out_far[512:])

    ins[0].wait()

    @pl.loop(0, 8)
    def _(i):
        h = x[rows(i, 64)].astype(f32) + wide[rows(i, 64)]
        hidden[rows(i, 64)] = h
        n[rows(i, 64)] = (h * norm_scale(h) * gain[8:9]).astype(low)

    outs[2].start()
    outs[3].start()
    ins[1].wait()
    n_own, n_far = n[:, lanes(row, 512)], n[:, lanes(1 - row, 512)]
    gate[...] = mm(n_own, gu_own[0]) + mm(n_far, gu_far[0])
    up[...] = mm(n_own, gu_own[1]) + mm(n_far, gu_far[1])
    ins[2].wait()
    dact[...] = mm_t(df[:, lanes(row, 512)], down_own[...]) + mm_t(df[:, lanes(1 - row, 512)], down_far[...])
    lane = lax.broadcasted_iota(jnp.int32, (64, 640), 1) - 64 * xl
    mine = (lane >= 0) & (lane < 576)

    @pl.loop(0, 8)
    def _(i):
        at = rows(i, 64)
        g = jnp.where(mine, gate[at], 0.0)
        v = jnp.where(mine, up[at], 0.0)
        da = dact[at]
        s = 1.0 / (1.0 + jnp.exp(-g))
        gs = g * s
        act[at] = (gs * v).astype(low)
        dgate[at] = (da * v * s * (1.0 + g * (1.0 - s))).astype(low)
        dup[at] = (da * gs).astype(low)

    for k, w in ((0, gu_own), (1, gu_far)):
        wide[:, 512 * k : 512 * k + 512] = mm_t(dgate[...], w[0]) + mm_t(dup[...], w[1])
    part(wide, keep, send, col)
    for copy in outs:
        copy.wait()


def part(wide, keep, send, col):
    for k in range(4):
        here = slice(256 * (k & 1), 256 * (k & 1) + 256)
        keep[k] = wide[here, lanes(2 * (k >> 1) + col, 256)]
        send[k, :256] = wide[here, lanes(2 * (k >> 1) + 1 - col, 256)].astype(low)


def feed_out(place, act, down_own, down_far, keep, send, wide):
    for k, w in ((0, down_own), (1, down_far)):
        wide[:, 512 * k : 512 * k + 512] = mm(act[...], w[...])
    part(wide, keep, send, place[2])


def source_row(m, half):
    return 128 * (m // 4) + 64 * half + 16 * (m % 4)


def feed_weights(place, n_in, act, dgate_in, dup_in, df, early_out, wide, early, n, dgate, dup, sems):
    xl = place[1]
    ins = [
        pltpu.make_async_copy(a, b, sems.at[i])
        for i, (a, b) in enumerate(((n_in, n), (dgate_in, dgate), (dup_in, dup)))
    ]
    spans = [pl.ds(640, 320)] + [pl.ds((2 * r + k) * 160, 160) for k in (0, 1) for r in (0, 1)]
    outs = [
        pltpu.make_async_copy(early.at[:, span], early_out.at[:, span], sems.at[3 + i])
        for i, span in enumerate(spans)
    ]
    for copy in ins:
        copy.start()
    wide[...] = mm(act[...].T, df[...])
    for i in range(8):
        some = wide[pl.ds(pl.multiple_of(64 * xl + 72 * i, 8), 72)]
        some = jnp.concatenate([some, jnp.zeros((8, 1024), f32)]).astype(low)
        for r in (0, 1):
            for t in range(4):
                early[8 * r + i, 640 + 80 * t : 720 + 80 * t] = some[:, 512 * r + 128 * t : 512 * r + 128 * t + 128]
    outs[0].start()
    for copy in ins:
        copy.wait()
    n_t = n[...].T
    for k, g in ((0, dgate), (1, dup)):
        for r in (0, 1):
            total = mm(n_t[512 * r : 512 * r + 512], g[...]).astype(low)
            for m in range(16):
                for t in range(5):
                    for h in (0, 1):
                        at = ((r * 2 + k) * 5 + t) * 32 + 16 * h
                        first = source_row(m, h)
                        early[m, at : at + 16] = total[first : first + 16, 128 * t : 128 * t + 128]
            outs[1 + 2 * k + r].start()
    for copy in outs:
        copy.wait()


def fold(place, keep, got, own, *others):
    own[...] = keep[0] + got[0].astype(f32)
    for k in (1, 2, 3):
        others[k - 1][...] = (keep[k] + got[k].astype(f32)).astype(low)


def mix_backward(place, *refs):
    near, far = refs[0:4], refs[4:8]
    hidden, df, gain, w_own, w_far, c, conv, same_one, same_two = refs[8:17]
    dh_own, do, dconv, dc, heads, head, dg_two = refs[17:24]
    (dn,) = refs[24:]
    row, xl, col = place[0], place[1], place[2]
    assemble(dn, row, col, near, far)
    own = lanes(2 * row + col, 256)
    dg_two[...] = jnp.zeros((8, 256), f32)

    @pl.loop(0, 8)
    def _(i):
        at = rows(i, 64)
        h = hidden[at]
        r = norm_scale(h)
        d = dn[at].astype(f32)
        scaled = d * gain[8:9]
        total = jnp.sum(scaled * h, axis=1, keepdims=True)
        dh = df[at].astype(f32) + r * scaled - h * (r * r * r * total / 1024)
        do[at] = dh.astype(low)

        @pl.when(i < 4)
        def _():
            h = hidden[at, own]
            d = dn[at, own].astype(f32)
            dh_own[at] = df[at, own].astype(f32) + r * d * gain[8:9, own] - h * (r * r * r * total / 1024)
            dg_two[...] += jnp.broadcast_to(jnp.sum(d * h * r, axis=0, keepdims=True), (8, 256))

    dy = mm_t(do[:, lanes(row, 512)], w_own[...]) + mm_t(do[:, lanes(1 - row, 512)], w_far[...])
    edge = dy * c[...]
    dconv[...] = edge
    dc[...] = dy * conv[...]
    ends = [
        jnp.concatenate([edge[at : at + 8] * same_one[at : at + 8], edge[at : at + 8] * same_two[at : at + 8]])
        for at in (0, 256)
    ]
    first = xl == 0
    heads[0] = jnp.where(first, ends[0], ends[1])
    heads[1] = jnp.where(first, ends[1], ends[0])
    head[...] = jnp.where(first, ends[0], ends[1])


def conv_backward(place, *refs):
    dconv, dc, later, last, same_one, same_two, taps, b, c, u, past_one, past_two, bx, w_own, w_far = refs[:15]
    x, scale, dg_two = refs[15:18]
    dproj, keep, send, total, small = refs[18:23]
    (wide,) = refs[23:]
    row, xl, col, zz = place[0], place[1], place[2], place[4]
    end = zz == 3
    rim = jnp.where(end, later[1], later[0]), jnp.where(end, last[...], later[1])
    parts = []
    for i in (0, 1):
        here = slice(256 * i, 256 * i + 256)
        d = dconv[here]
        edge = jnp.where(xl == i, rim[0], rim[1])
        one = jnp.concatenate([d * same_one[here], edge[:8]])
        two = jnp.concatenate([d * same_two[here], edge[8:]])
        dbx = taps[2:3] * d + taps[1:2] * one[1:257] + taps[0:1] * two[2:258]
        parts.append(jnp.concatenate([
            jnp.sum(d * past_two[here], axis=0, keepdims=True),
            jnp.sum(d * past_one[here], axis=0, keepdims=True),
            jnp.sum(d * bx[here].astype(f32), axis=0, keepdims=True),
            jnp.zeros((5, 128), f32),
        ]))
        db = (dbx * u[here]).astype(low)
        dcv = dc[here].astype(low)
        du = (dbx * b[here]).astype(low)
        dproj[here, 0:128] = db
        dproj[here, 128:256] = dcv
        dproj[here, 256:384] = du
        mass = jnp.sum(
            db.astype(f32) * b[here] + dcv.astype(f32) * c[here] + du.astype(f32) * u[here], axis=1, keepdims=True
        )
        line = jnp.broadcast_to(mass, (256, 128)).T[:8]
        total[i] = line
        high = line.astype(low)
        rest = (line - high.astype(f32)).astype(low)
        both = jnp.concatenate([high, rest])
        send[i, 256:272] = both
        send[2 + i, 256:272] = both
    zero = jnp.zeros((1, 128), f32)
    for k, w in ((0, w_own), (1, w_far)):
        whole = jnp.concatenate([w[0], w[1], w[2]], axis=1)
        wide[:, 512 * k : 512 * k + 512] = mm_t(dproj[...], whole)
        sums = jnp.zeros((1, 512), f32)
        for i in range(8):
            here = slice(64 * i, 64 * i + 64)
            v = x[here, lanes(row ^ k, 512)].astype(f32)
            r = scale[here]
            r = jnp.concatenate([r, r, r, r], axis=1)
            sums += jnp.sum(wide[here, 512 * k : 512 * k + 512] * v * r, axis=0, keepdims=True)
        lines = [sums[:, 128 * t : 128 * t + 128] for t in range(4)]
        if k == 0:
            lines += [dg_two[0:1, :128], dg_two[0:1, 128:]]
            for a in range(3):
                tap = parts[0][a : a + 1] + parts[1][a : a + 1]
                lines += [jnp.where(xl == 0, tap, zero), jnp.where(xl == 0, zero, tap)]
        lines += [zero] * (16 - len(lines))
        small[row ^ k] = jnp.concatenate(lines).astype(low)
    part(wide, keep, send, col)


def mix_weights(place, n, dproj, y, do, small, late):
    n_t = n[...].T
    for r in (0, 1):
        total = mm(n_t[512 * r : 512 * r + 512], dproj[...]).astype(low)
        for m in range(16):
            for h in (0, 1):
                for k in range(3):
                    first = source_row(m, h)
                    at = 48 * (2 * r + h) + 16 * k
                    late[m, at : at + 16] = total[first : first + 16, 128 * k : 128 * k + 128]
            late[m, 256 + 16 * r : 272 + 16 * r] = small[r]
    total = mm(y[...].T, do[...]).astype(low)
    for r in (0, 1):
        for i in range(8):
            for t in range(4):
                late[8 * r + i, 192 + 16 * t : 208 + 16 * t] = total[
                    16 * i : 16 * i + 16, 512 * r + 128 * t : 512 * r + 128 * t + 128
                ]


def fold_last(place, keep, got, keep_ffn, got_ffn, total, own, own_ffn, mass, *others):
    for k in range(4):
        whole = keep[k] + got[k, :256].astype(f32)
        line = total[k & 1] + got[k, 256:264].astype(f32) + got[k, 264:272].astype(f32)
        ffn = keep_ffn[k] + got_ffn[k].astype(f32)
        if k == 0:
            own[...] = whole
            own_ffn[...] = ffn
            mass[...] = line
        else:
            others[k - 1][272:528] = ffn.astype(low)
            others[k - 1][:256] = whole.astype(low)
            high = line.astype(low)
            others[k - 1][256:272] = jnp.concatenate([high, (line - high.astype(f32)).astype(low)])


def finish(place, own, own_ffn, mass, got1, got2, got3, dh, hidden, x, gain, out, mixed):
    row, col = place[0], place[2]
    here = lanes(2 * row + col, 256)
    total, line, ffn = own[...], mass[...], own_ffn[...]
    for got in (got1, got2, got3):
        total += got[:256].astype(f32)
        ffn += got[272:528].astype(f32)
        line += got[256:264].astype(f32) + got[264:272].astype(f32)
    scale = norm_scale(x[:256].astype(f32))
    column = turn(line[0:1])
    column = jnp.concatenate([column, column], axis=1)
    v = x[:256, here].astype(f32)
    mixed[...] = (hidden[...] + ffn).astype(low)
    out[...] = (dh[...] + scale * gain[0:1, here] * total - v * (scale * scale) * column / 1024).astype(low)


def deal(place, late, early, settled, *messages):
    row, xl = place[0], place[1]

    def total(here):
        parts = [late[m, here].astype(f32) for m in range(16)]
        while len(parts) > 1:
            parts = [a + b for a, b in zip(parts[::2], parts[1::2])]
        return parts[0].astype(low)

    for j, message in enumerate(messages):
        r, half = row ^ (j >> 1), xl ^ (j & 1)
        message[0:48] = total(pl.ds(pl.multiple_of(48 * (2 * r + half), 16), 48))
        message[48:64] = total(rows(16 + r, 16))
        for i in range(10):
            message[64 + 16 * i : 80 + 16 * i] = early[pl.ds(pl.multiple_of((10 * r + i) * 32 + 16 * half, 16), 16)]
    settled[0:64] = total(slice(192, 256))
    settled[64:384] = early[640:960]


def place_out(place, settled, m0, m1, m2, m3, g_in, g_out, g_gu, g_down):
    spot = 2 * place[0] + place[1]
    got = (m0, m1, m2, m3)

    def sender(q, here):
        return jnp.where(
            spot == q,
            got[0][here],
            jnp.where(spot == (q ^ 1), got[1][here], jnp.where(spot == (q ^ 2), got[2][here], got[3][here])),
        ).astype(f32)

    for q in range(4):
        whole = sender(q, slice(None))
        for k in range(3):
            g_in[k, :, 128 * q : 128 * q + 128] = whole[16 * k : 16 * k + 16]
        first = 9 * q // 2
        for k in (0, 1):
            for t in range(5):
                at = 64 + 16 * (5 * k + t)
                here = slice(128 * (first + t), 128 * (first + t) + 128)
                if q % 2 and t == 0:
                    g_gu[:, k, here] += whole[at : at + 16]
                else:
                    g_gu[:, k, here] = whole[at : at + 16]
    for t in range(4):
        here = slice(128 * t, 128 * t + 128)
        g_out[:, here] = settled[16 * t : 16 * t + 16].astype(f32)
        g_down[:, here] = settled[64 + 80 * t : 144 + 80 * t].astype(f32)[:72]


def local(
    tokens,
    segment_ids,
    gain_one,
    in_weight,
    conv_weight,
    out_weight,
    gain_two,
    gate_up,
    down_weight,
    cotangent,
):
    yy, xl, zz, row, col = (lax.axis_index(a) for a in AXES)
    q = 2 * row + xl
    place = jnp.stack([row, xl, col, yy, zz]).astype(jnp.int32)

    def cut(value, index, size, axis):
        return lax.dynamic_slice_in_dim(value, index * size, size, axis)

    def window(value, index, axis):
        return lax.dynamic_slice_in_dim(value, (9 * index // 2) * 128, 640, axis)

    extra = []
    for gain in (gain_one, gain_two):
        for _ in range(3):
            piece = lax.reduce_precision(gain, 8, 7)
            extra.append(piece)
            gain = gain - piece
    extra.append(segment_ids.astype(f32))
    extra = jnp.pad(jnp.stack(extra), ((0, 9), (0, 0))).astype(low)
    piece = jnp.concatenate([tokens, extra])
    in_w = in_weight.transpose(1, 0, 2)
    in_own, in_send = cut(in_w, q, 128, 2), cut(in_w, 3 - q, 128, 2)
    in_send = jnp.concatenate([in_send[:, :256], in_send[:, 256:]], axis=2).reshape(768, 256)
    near = [piece, ring(piece, 1), ring(piece, 2), ring(jnp.concatenate([piece, in_send]), 3)]
    taps = jnp.pad(cut(conv_weight, xl, 128, 0).T.astype(f32), ((0, 5), (0, 0)))

    def begin(index):
        return (9 * index // 2) * 128

    m = 4 * yy + zz
    gu_part = lax.dynamic_slice(gate_up, (32 * m, 0, begin(3 - q)), (32, 2, 640))
    gu_part = gu_part.reshape(32, 2, 5, 128).transpose(1, 2, 0, 3).reshape(320, 128)
    down_part = lax.dynamic_slice(down_weight, (begin(3 - q) + 16 * (5 * m // 2), 0), (48, 512))
    down_part = down_part.reshape(48, 4, 128).transpose(1, 0, 2).reshape(192, 128)
    out_part = cut(out_weight, m, 32, 0).reshape(32, 4, 128).transpose(1, 0, 2).reshape(128, 128)
    pack = ring(jnp.concatenate([gu_part, down_part, out_part]), 3)
    cross = moved(out_part, ("xl", "row", "col"), lambda xl, row, col: (1 - xl, 1 - row, 1 - col))
    packs = lax.all_gather(jnp.concatenate([pack, cross]), ("y", "z"))
    out_swap = swap_core(out_weight)
    gu_own, down_own = window(gate_up.transpose(1, 0, 2), q, 2), window(down_weight, q, 0)

    out_line = cut(out_weight, q, 128, 0)
    in_own, gu_own, down_own, taps, out_line, place, near[1] = lax.optimization_barrier(
        (in_own, gu_own, down_own, taps, out_line, place, near[1])
    )
    far = [swap_core(v) for v in near[:3]] + [swap_core(near[3][:272])]
    tile = shaped(512, 128)
    tile_low = shaped(512, 128, kind=low)
    whole_low = shaped(512, 1024, kind=low)
    x, n_one, gain, b, c, u, bx, tails, tail, same_one, same_two, scale = call(
        front,
        [
            whole_low,
            whole_low,
            shaped(16, 1024),
            tile,
            tile,
            tile,
            tile_low,
            shaped(2, 8, 128),
            shaped(8, 128),
            tile,
            tile,
            tile,
        ],
        [pltpu.VMEM((3, 512, 128), low)],
        place,
        *near,
        *far,
        in_own,
    )
    in_far = near[3][272:].reshape(3, 256, 2, 128).transpose(0, 2, 1, 3).reshape(3, 512, 128)
    df, tails = lax.optimization_barrier((cotangent, tails))
    df_near = [df] + [ring(df, k) for k in (1, 2, 3)]
    df_far = [swap_core(v) for v in df_near]
    prior = moved(tails, ("z",), lambda z: ((z + 1) % 4,))
    first = moved(tail, ("y", "z"), lambda y, z: (y + 1, 0) if z == 3 and y < 3 else None)
    conv, y, y_swap, past_one, past_two = call(
        conv_forward, [tile, tile_low, tile_low, tile, tile], [], place, bx, prior, first, c, same_one, same_two, taps
    )
    near = [y, ring(y_swap, 1), ring(y, 2), ring(y_swap, 3)]
    far = [swap_core(v) for v in near]

    hid_low = shaped(512, 640, kind=low)
    keep4, send4 = shaped(4, 256, 256), shaped(4, 256, 256, kind=low)
    send4_mass = shaped(4, 272, 256, kind=low)
    hidden, n_two, act, dgate, dup, keep, send, df, down_far, out_row = call(
        feed,
        [
            shaped(512, 1024),
            whole_low,
            hid_low,
            hid_low,
            hid_low,
            keep4,
            send4,
            whole_low,
            shaped(640, 512, kind=low),
            shaped(128, 512, kind=low),
        ],
        [
            pltpu.VMEM((512, 1024), low),
            pltpu.VMEM((512, 1024), f32),
            pltpu.VMEM((512, 640), f32),
            pltpu.VMEM((512, 640), f32),
            pltpu.VMEM((512, 640), f32),
            pltpu.VMEM((2, 512, 640), low),
            pltpu.VMEM((1024, 512), low),
            pltpu.VMEM((512, 1024), low),
            pltpu.VMEM((2, 512, 640), low),
            pltpu.VMEM((640, 512), low),
            pltpu.VMEM((512, 1024), f32),
            pltpu.VMEM((512, 1024), low),
            pltpu.VMEM((512, 1024), low),
            pltpu.VMEM((640, 512), low),
            pltpu.SemaphoreType.DMA((7,)),
        ],
        place,
        *near,
        *far,
        x,
        gain,
        out_weight,
        out_swap,
        gu_own,
        down_own,
        *df_near,
        *df_far,
        packs,
        loose_in=(8, 12, 13),
        loose_out=(0, 1, 7, 8),
    )
    got = swap_core(send)
    own = shaped(256, 256)
    own_low = shaped(256, 256, kind=low)
    dn_own, *parts = call(fold, [own, own_low, own_low, own_low], [], place, keep, got)
    ringed = [ring(v, k) for k, v in zip((1, 2, 3), parts)]
    (early,) = call(
        feed_weights,
        [shaped(16, 960, 128, kind=low)],
        [
            pltpu.VMEM((640, 1024), f32),
            pltpu.VMEM((16, 960, 128), low),
            pltpu.VMEM((512, 1024), low),
            pltpu.VMEM((512, 640), low),
            pltpu.VMEM((512, 640), low),
            pltpu.SemaphoreType.DMA((8,)),
        ],
        place,
        n_two,
        act,
        dgate,
        dup,
        df,
        loose_in=(0, 2, 3),
        loose_out=(0,),
    )
    dn_own, early = lax.optimization_barrier((dn_own, early))
    early = early.reshape(16 * 960, 128)
    early = lax.psum_scatter(early, ("y", "z"), scatter_dimension=0, tiled=True)
    piece = (dn_own + sum(v.astype(f32) for v in ringed)).astype(low)
    near = [piece] + [ring(piece, k) for k in (1, 2, 3)]
    far = [swap_core(v) for v in near]
    dh_own, do, dconv, dc, heads, head, dg_two = call(
        mix_backward,
        [own, whole_low, tile, tile, shaped(2, 16, 128), shaped(16, 128), shaped(8, 256)],
        [pltpu.VMEM((512, 1024), low)],
        place,
        *near,
        *far,
        hidden,
        df,
        gain,
        out_line,
        out_row,
        c,
        conv,
        same_one,
        same_two,
    )
    act, heads = lax.optimization_barrier((act, heads))
    keep_ffn, send_ffn = call(
        feed_out, [keep4, send4], [pltpu.VMEM((512, 1024), f32)], place, act, down_own, down_far
    )
    dconv, send_ffn = lax.optimization_barrier((dconv, send_ffn))
    got_ffn = swap_core(send_ffn)
    later = moved(heads, ("z",), lambda z: ((z - 1) % 4,))
    last = moved(head, ("y", "z"), lambda y, z: (y - 1, 3) if z == 0 and y > 0 else None)
    dproj, keep, send, total, small = call(
        conv_backward,
        [shaped(512, 384, kind=low), keep4, send4_mass, shaped(2, 8, 256), shaped(2, 16, 128, kind=low)],
        [pltpu.VMEM((512, 1024), f32)],
        place,
        dconv,
        dc,
        later,
        last,
        same_one,
        same_two,
        taps,
        b,
        c,
        u,
        past_one,
        past_two,
        bx,
        in_own,
        in_far,
        x,
        scale,
        dg_two,
    )
    got = swap_core(send)
    own_mass = shaped(528, 256, kind=low)
    dn_own, ffn_own, mass, *parts = call(
        fold_last,
        [own, own, shaped(8, 256), own_mass, own_mass, own_mass],
        [],
        place,
        keep,
        got,
        keep_ffn,
        got_ffn,
        total,
    )
    (late,) = call(mix_weights, [shaped(16, 288, 128, kind=low)], [], place, n_one, dproj, y, do, small)
    ringed = [ring(v, k) for k, v in zip((1, 2, 3), parts)]
    late = lax.all_to_all(late, ("y", "z"), 0, 0)
    h_own = lax.dynamic_slice_in_dim(hidden[:256], (2 * row + col) * 256, 256, 1)
    grad_tokens, mixed = call(
        finish, [own_low, own_low], [], place, dn_own, ffn_own, mass, *ringed, dh_own, h_own, x, gain
    )

    late, grad_tokens, mixed = lax.optimization_barrier((late, grad_tokens, mixed))

    settled, *messages = call(
        deal, [shaped(384, 128, kind=low)] + [shaped(224, 128, kind=low)] * 4, [], place, late, early
    )
    settled = moved(
        settled, ("y", "xl", "z", "row"), lambda y, xl, z, r: (2 * r + xl, y % 2, z, y // 2)
    )
    messages = [messages[0]] + [ring(messages[k], k) for k in (1, 2, 3)]
    extra = sum(message[48:64].astype(f32) for message in messages)
    mine, cross = by_core(col, extra[0:2], extra[2:4])
    cross, settled = lax.optimization_barrier((cross, settled))
    cross = swap_core(cross)
    grad_in, grad_out, grad_gate_up, grad_down = call(
        place_out,
        [shaped(3, 16, 512), shaped(16, 512), shaped(16, 2, 2304), shaped(72, 512)],
        [],
        place,
        settled,
        *messages,
    )
    small = jnp.concatenate([mine + cross, extra[4:12]]).reshape(5, 256)
    small = cut(small, 8 * yy + 4 * xl + zz, 8, 1)
    return (
        mixed,
        grad_tokens,
        small[0],
        grad_in.transpose(1, 0, 2),
        small[2:5].T,
        grad_out,
        small[1],
        grad_gate_up,
        grad_down,
    )


def solution(mesh):
    dp = ("y", "xl", "z")
    fine = Mesh(mesh.devices.reshape(tuple(SIZES.values())), AXES)
    return jax.shard_map(
        local,
        mesh=fine,
        in_specs=(
            P(dp, ("row", "col")),
            P(dp),
            P(("row", "col")),
            P("row", None, "col"),
            P(("col", "row"), None),
            P("col", "row"),
            P(("row", "col")),
            P("row", None, "col"),
            P("col", "row"),
            P(dp, ("row", "col")),
        ),
        out_specs=(
            P(dp, ("row", "col")),
            P(dp, ("row", "col")),
            P(("row", "col", *dp)),
            P(("row", *dp), None, "col"),
            P(("col", "row", *dp), None),
            P(("col", *dp), "row"),
            P(("row", "col", *dp)),
            P(("row", *dp), None, "col"),
            P(("col", *dp), "row"),
        ),
        check_vma=False,
    )
```
